768 devices in a mesh: seq: 96 (over y, z), head: 8 (over x, core).
Axes of the slice: x: 4, y: 8, z: 12, core: 2. Of those that a mesh axis runs over, the one named last changes fastest.
Arguments:
- hidden: bfloat16 [12288, 2048], P('seq', 'head'), may hold values from -6 to 6
- beta_weight: bfloat16 [2048, 16], P('head'), may hold values from -0.125 to 0.125
- beta_bias: float32 [16], P('head'), as said below
- queries: bfloat16 [12288, 2048], P('seq', 'head'), may hold values from -6 to 6
- keys: bfloat16 [12288, 2048], P('seq', 'head'), may hold values from -6 to 6
- values: bfloat16 [12288, 2048], P('seq', 'head'), may hold values from -6 to 6
- cotangent: bfloat16 [12288, 2048], P('seq', 'head'), may hold values from -6 to 6
Outputs:
- layer_out: bfloat16 [12288, 2048], P('seq', 'head')
- d_queries: bfloat16 [12288, 2048], P('seq', 'head')
- d_keys: bfloat16 [12288, 2048], P('seq', 'head')
- d_values: bfloat16 [12288, 2048], P('seq', 'head')
- d_hidden: bfloat16 [12288, 2048], P('seq', 'head')
- d_weight: float32 [2048, 16], P('head')
- d_bias: float32 [16], P('head')
The draws below stay inside these ranges and needn't reach their ends.
Inputs may be any that keep to these rules, and one draw needn't show every extreme that they name: `beta_bias`: at most ln(768) + 1.
All inputs are finite; a program needn't handle non-finite values.
Results may differ from the reference program's by a relative error of at most 0.006.
Values may be sent and summed in bfloat16 or wider, within the bound.
No kernel may reach another device: no remote copies, remote signals or barrier semaphores. Data moves between devices by JAX's collectives and lax.ppermute only.
A program may use at most 128 MiB of HBM per device.

```python
import math
import jax
import jax.numpy as jnp
from jax import lax

HEAD_DIM = 128
HEADS = 16
WIDTH = 2048
TOK_DEV = 128
TOKENS = 12288


def draw_beta_bias(key, part):
    key_mask, key_slow, key_fast = jax.random.split(key, 3)
    slow_share = 0.5
    chosen = jax.random.uniform(key_mask, (HEADS,), jnp.float32) < slow_share
    slow_level = jnp.log(8.0 * TOKENS / HEAD_DIM) + jax.random.uniform(key_slow, (HEADS,), jnp.float32, -0.5, 1.0)
    fast_level = jax.random.uniform(key_fast, (HEADS,), jnp.float32, -6.0, -4.0)
    return jnp.where(chosen, slow_level, fast_level).astype(jnp.float32)


def steps_of(rng, shape, cuts, low, largest):
    loudness, own = 1.0, jax.random.fold_in(rng, 6)
    for position, parts in cuts:
        steps = jnp.exp(jax.random.uniform(jax.random.fold_in(own, position), (parts,), jnp.float32, low / len(cuts), largest / len(cuts)))
        loudness = loudness * jnp.repeat(steps, shape[position] // parts).reshape([-1 if axis == position else 1 for axis in range(len(shape))])
    return loudness


def scatter_about(own_key, dims, scale, limit, shards=(), held_as=jnp.bfloat16):
    values = jax.random.normal(own_key, dims, jnp.float32) * scale
    if len(shards) > 0:
        values = steps_of(own_key, dims, shards, -0.22, 0.18) * values
    return jnp.clip(values, min=-limit, max=limit).astype(held_as)


def setup_inputs(seed: int = 0) -> dict:
    streams_of = jax.random.split(jax.random.key(seed), 8)
    hidden = scatter_about(streams_of[0], (TOKENS, WIDTH), 1.0, 6.0, ((0, 96), (1, 8)))
    beta_weight = scatter_about(streams_of[1], (WIDTH, HEADS), WIDTH ** -0.5, 0.125, ((0, 8),))
    beta_bias = draw_beta_bias(jax.random.fold_in(streams_of[7], 71), 0)
    queries = scatter_about(streams_of[3], (TOKENS, WIDTH), 1.0, 6.0, ((0, 96), (1, 8)))
    keys = scatter_about(streams_of[4], (TOKENS, WIDTH), 1.0, 6.0, ((0, 96), (1, 8)))
    values = scatter_about(streams_of[5], (TOKENS, WIDTH), 1.0, 6.0, ((0, 96), (1, 8)))
    cotangent = scatter_about(streams_of[6], (TOKENS, WIDTH), 1.0, 6.0, ((0, 96), (1, 8)))
    return dict(hidden=hidden, beta_weight=beta_weight, beta_bias=beta_bias, queries=queries, keys=keys, values=values, cotangent=cotangent)


HIGHEST = lax.Precision.HIGHEST

def normalize(vectors):
    return vectors / jnp.sqrt(lax.optimization_barrier(jnp.sum(vectors * vectors, axis=-1, keepdims=True)) + 1e-06)

def prepare(queries_f, keys_f, logits):
    return (normalize(queries_f), normalize(keys_f), 2.0 * jax.nn.sigmoid(logits))

def token_step(memory, pieces):
    query_t, key_t, value_t, beta_t = pieces
    recalled = jnp.einsum('hrd,hd->hr', memory, key_t, precision=HIGHEST)
    memory = memory + beta_t[:, None, None] * (value_t - recalled)[:, :, None] * key_t[:, None, :]
    output = jnp.einsum('hrd,hd->hr', memory, query_t, precision=HIGHEST)
    return (memory, output)

def sequence_outputs(queries_n, keys_n, values_f, betas):
    inner_len = math.gcd(TOK_DEV, 64)
    outer_len = TOKENS // TOK_DEV
    inside_len = TOK_DEV // inner_len

    def inner_scan(memory, pieces):
        return lax.scan(token_step, memory, pieces)

    def outer_scan(memory, pieces):
        return lax.scan(jax.checkpoint(inner_scan), memory, pieces)

    def blocked(array):
        return array.reshape((outer_len, inside_len, inner_len) + array.shape[1:])
    start_state = jnp.zeros((HEADS, HEAD_DIM, HEAD_DIM), jnp.float32)
    unused, outputs = lax.scan(jax.checkpoint(outer_scan), start_state, (blocked(queries_n), blocked(keys_n), blocked(values_f), blocked(betas)))
    raw_out = outputs.reshape(TOKENS, HEADS, HEAD_DIM)
    return raw_out / jnp.sqrt(lax.optimization_barrier(jnp.mean(raw_out * raw_out, axis=-1, keepdims=True)) + 1e-05)

def reference(hidden, beta_weight, beta_bias, queries, keys, values, cotangent):
    logits = jnp.dot(hidden, beta_weight, preferred_element_type=jnp.float32) + beta_bias[None, :]

    def shaped(array):
        return array.astype(jnp.float32).reshape(TOKENS, HEADS, HEAD_DIM)
    (queries_n, keys_n, betas), prep_pullback = jax.vjp(prepare, shaped(queries), shaped(keys), logits)
    normed, pullback = jax.vjp(sequence_outputs, queries_n, keys_n, shaped(values), betas)
    grads_n = pullback(shaped(cotangent))
    d_queries_f, d_keys_f, d_logits = prep_pullback((grads_n[0], grads_n[1], grads_n[3]))
    grad_rounded = d_logits.astype(jnp.bfloat16)
    d_hidden = jnp.dot(grad_rounded, beta_weight.T, preferred_element_type=jnp.float32).astype(jnp.bfloat16)
    d_weight = jnp.dot(hidden.T, grad_rounded, preferred_element_type=jnp.float32)
    d_bias = lax.optimization_barrier(jnp.sum(d_logits, axis=0))

    def flatten_out(array):
        return array.reshape(TOKENS, WIDTH).astype(jnp.bfloat16)
    return (flatten_out(normed), flatten_out(d_queries_f), flatten_out(d_keys_f), flatten_out(grads_n[2]), d_hidden, d_weight, d_bias)
```

```python
import functools

import jax
import jax.numpy as jnp
from jax import lax
from jax.experimental import pallas as pl
from jax.experimental.pallas import tpu as pltpu
from jax.sharding import Mesh, PartitionSpec as P

F32 = jnp.float32
BF16 = jnp.bfloat16
L = 128
D = 128
NN = (((1,), (0,)), ((), ()))
NT = (((1,), (1,)), ((), ()))
TN = (((0,), (0,)), ((), ()))


def dot1(a, b, dims=NN):
    return lax.dot_general(a, b, dims, preferred_element_type=F32)


def split(x):
    hi = x.astype(BF16)
    return hi, (x - hi.astype(F32)).astype(BF16)


def dot2(a, b, dims=NN):
    hi, lo = split(a)
    return dot1(hi, b, dims) + dot1(lo, b, dims)


def dot2r(a, b, dims=NN):
    hi, lo = split(b)
    return dot1(a, hi, dims) + dot1(a, lo, dims)


def dot3(a, b, dims=NN):
    ah, al = split(a)
    bh, bl = split(b)
    return dot1(ah, bh, dims) + (dot1(al, bh, dims) + dot1(ah, bl, dims))


def index_grids():
    row = lax.broadcasted_iota(jnp.int32, (L, L), 0)
    col = lax.broadcasted_iota(jnp.int32, (L, L), 1)
    return row, col


def to_col(row_vec, row, col):
    return jnp.sum(jnp.where(row == col, row_vec, 0.0), axis=1, keepdims=True)


def to_row(col_vec, row, col):
    return jnp.sum(jnp.where(row == col, col_vec, 0.0), axis=0, keepdims=True)


def inv_norm(raw):
    f = raw.astype(F32)
    return lax.rsqrt(jnp.sum(f * f, axis=1, keepdims=True) + 1e-06)


def triangle_inverse(strict, row, col):
    eye = jnp.where(row == col, 1.0, 0.0)
    diff = row ^ col
    inv = eye - jnp.where(diff == 1, strict, 0.0)
    size = 2
    while size < L:
        below = jnp.where((diff >= size) & (diff < 2 * size), strict, 0.0)
        inv = inv - dot3(inv, dot3(below, inv))
        size *= 2
    return inv


def block_prepare(kr, vr, logit_row):
    row, col = index_grids()
    beta_row = 2.0 * jax.nn.sigmoid(logit_row)
    beta = to_col(beta_row, row, col)
    rk = inv_norm(kr)
    rk_row = to_row(rk, row, col)
    gram = dot1(kr, kr, NT) * rk * rk_row
    strict = jnp.where(row > col, gram * beta_row, 0.0)
    inv = triangle_inverse(strict, row, col)
    solved_k = dot2(inv * rk_row, kr)
    solved_v = dot2(inv, vr)
    scale = beta * rk
    less = dot2(solved_k * scale, kr, TN)
    gain = dot2(solved_v * scale, kr, TN)
    back_k = dot3(inv, beta * (kr.astype(F32) * rk), TN)
    return less, gain, inv, solved_k, solved_v, back_k, gram


def block_outputs(qr, kr, ct, logit_row, start, inv, solved_k, solved_v):
    row, col = index_grids()
    beta = to_col(2.0 * jax.nn.sigmoid(logit_row), row, col)
    rk, rq = inv_norm(kr), inv_norm(qr)
    rk_row = to_row(rk, row, col)
    attend = jnp.where(row >= col, dot1(qr, kr, NT) * rq * rk_row, 0.0)
    errors = solved_v - dot3(solved_k, start, NT)
    scaled = beta * errors
    raw = rq * dot2r(qr, start, NT) + dot3(attend, scaled)
    rn = lax.rsqrt(jnp.mean(raw * raw, axis=1, keepdims=True) + 1e-05)
    normed = raw * rn
    cotan = ct.astype(F32)
    d_raw = rn * (cotan - normed * jnp.mean(normed * cotan, axis=1, keepdims=True))
    back0 = dot3(inv, beta * dot3(attend, d_raw, TN), TN)
    give = dot2(d_raw * rq, qr, TN) - dot2(back0 * rk, kr, TN)
    return normed, errors, d_raw, back0, give


def block_grads_early(qr, kr, logit_row, start, errors, d_raw):
    row, col = index_grids()
    beta = to_col(2.0 * jax.nn.sigmoid(logit_row), row, col)
    rk, rq = inv_norm(kr), inv_norm(qr)
    rk_row = to_row(rk, row, col)
    scaled = beta * errors
    d_attend = jnp.where(row >= col, dot3(d_raw, scaled, NT), 0.0)
    dq_unit = dot3(d_raw, start) + dot2(d_attend * rk_row, kr)
    dk_part = dot2(d_attend * rq, qr, TN)
    q_unit = qr.astype(F32) * rq
    dq = rq * (dq_unit - q_unit * jnp.sum(q_unit * dq_unit, axis=1, keepdims=True))
    return dq, dk_part


def block_grads(kr, logit_row, start, end_grad, errors, back0, back_k, dk_part):
    row, col = index_grids()
    beta = to_col(2.0 * jax.nn.sigmoid(logit_row), row, col)
    keep = to_col(jax.nn.sigmoid(-logit_row), row, col)
    rk = inv_norm(kr)
    rk_row = to_row(rk, row, col)
    scaled = beta * errors
    back = back0 + dot3(back_k, end_grad, NT)
    d_logit = to_row(jnp.sum(errors * back, axis=1, keepdims=True) * keep, row, col)
    d_gram = jnp.where(row > col, -dot3(back, scaled, NT), 0.0)
    d_gram = d_gram + jnp.where(row < col, -dot3(scaled, back, NT), 0.0)
    dk_unit = dk_part - dot3(back, start) + dot3(scaled, end_grad) + dot2(d_gram * rk_row, kr)
    k_unit = kr.astype(F32) * rk
    dk = rk * (dk_unit - k_unit * jnp.sum(k_unit * dk_unit, axis=1, keepdims=True))
    return dk, back, d_logit


def level_of(x):
    top = jnp.max(jnp.max(jnp.abs(x), axis=1, keepdims=True), axis=0, keepdims=True)
    return jnp.ceil(jnp.log2(jnp.maximum(top, 1e-30)))


def packed(x):
    level = level_of(x)
    return x * jnp.exp2(-level), jnp.broadcast_to(level, (16, D))


def scaled_back(x, level):
    return x * jnp.exp2(level[0:1])


def step(state, less, dims=NN):
    return state - dot3(state, less, dims)


def chain_forward(less, gain, place, count):
    eye = jnp.where(index_grids()[0] == index_grids()[1], 1.0, 0.0)
    zero = jnp.zeros((D, D), F32)
    state = jnp.concatenate([eye, zero], axis=0)
    own = state
    for j in range(count):
        own = jnp.where(place == j, state, own)
        if j == 0:
            state = jnp.concatenate([eye - less(j), gain(j)], axis=0)
        else:
            state = step(state, less(j)) + jnp.concatenate([zero, gain(j)], axis=0)
    return state, own


def chain_state(less, gain, place, count):
    state = jnp.zeros((D, D), F32)
    own = state
    for j in range(count - 1):
        state = gain(j) if j == 0 else step(state, less(j)) + gain(j)
        own = jnp.where(place == j + 1, state, own)
    return own


def chain_back_matrix(less, place, count):
    state = jnp.where(index_grids()[0] == index_grids()[1], 1.0, 0.0)
    own = state
    for j in range(count - 1, 0, -1):
        state = step(state, less(j), NT)
        own = jnp.where(place == j - 1, state, own)
    return own


def chain_back(less, give, place, count, total=True):
    state = jnp.zeros((D, D), F32)
    own = state
    for j in range(count - 1, -1 if total else 0, -1):
        own = jnp.where(place == j, state, own)
        state = give(j) if j == count - 1 else step(state, less(j), NT) + give(j)
    if not total:
        own = jnp.where(place == 0, state, own)
    return state, own


def put(send, less, gain):
    send[0:D] = less
    send[D : 2 * D], send[2 * D : 2 * D + 16] = packed(gain)


def less_of(got):
    return lambda j: got[j, 0:D]


def gain_of(got):
    return lambda j: scaled_back(got[j, D : 2 * D], got[j, 2 * D : 2 * D + 8])


def give_of(got):
    return lambda j: scaled_back(got[j, 0:D], got[j, D : D + 8])


def kernel_prepare(lg, kv, send, less, gain, inv, sk, sv, bk):
    moves = []
    for b in range(2):
        w, n, *rest, _ = block_prepare(kv[b, 0], kv[b, 1], lg[b : b + 1, :])
        less[b], gain[b] = w, n
        inv[b], sk[b], sv[b], bk[b] = rest
        moves.append((w, n))
    (w0, n0), (w1, n1) = moves
    both = step(jnp.concatenate([w0, n0], axis=0), w1)
    put(send, both[:D] + w1, both[D:] + n1)


def kernel_row_forward(count, place, got, send, own):
    state, before = chain_forward(less_of(got), gain_of(got), place[0], count)
    row, col = index_grids()
    put(send, jnp.where(row == col, 1.0, 0.0) - state[:D], state[D:])
    own[...] = before


def kernel_row_matrix(count, place, got, own):
    own[...] = chain_back_matrix(less_of(got), place[0], count)


def kernel_outputs(count, place, got, own, lg, kv, qc, less, gain, inv, sk, sv,
                   out, start, err, draw, back0, give, send):
    first = chain_state(less_of(got), gain_of(got), place[0], count)
    before = dot3(first, own[:D]) + own[D:]
    gives = []
    for b in range(2):
        if b == 1:
            before = step(before, less[0]) + gain[0]
        normed, e, dr, b0, g = block_outputs(
            qc[b, 0], kv[b, 0], qc[b, 1], lg[b : b + 1, :], before, inv[b], sk[b], sv[b]
        )
        out[b] = normed.astype(BF16)
        start[b], err[b], draw[b], back0[b] = before, e, dr, b0
        gives.append(g)
    give[...] = gives[1]
    send[0:D], send[D : D + 16] = packed(step(gives[1], less[0], NT) + gives[0])


def kernel_early(lg, kv, qc, start, err, draw, dq, dkp):
    for b in range(2):
        x, y = block_grads_early(
            qc[b, 0], kv[b, 0], lg[b : b + 1, :], start[b], err[b], draw[b]
        )
        dq[b] = x.astype(BF16)
        dkp[b] = y


def kernel_row_back(count, place, got, gives, send, own):
    state, after = chain_back(less_of(got), give_of(gives), place[0], count)
    send[0:D], send[D : D + 16] = packed(state)
    own[...] = after


def kernel_grads(count, place, got, gives, matrix, own, lg, kv, less, give, start, err,
                 back0, bk, dkp, dkv, dlog):
    _, row_after = chain_back(less_of(got), give_of(gives), place[0], count, total=False)
    end_grad = dot3(row_after, matrix[...]) + own[...]
    for b in (1, 0):
        if b == 0:
            end_grad = step(end_grad, less[1], NT) + give[...]
        x, y, z = block_grads(
            kv[b, 0], lg[b : b + 1, :], start[b], end_grad, err[b], back0[b], bk[b], dkp[b]
        )
        dkv[b, 0], dkv[b, 1] = x.astype(BF16), y.astype(BF16)
        dlog[b : b + 1, :] = z


VM = pl.BlockSpec(memory_space=pltpu.VMEM)
SM = pl.BlockSpec(memory_space=pltpu.SMEM)


def call(body, outs, *args, flops=1e8):
    specs = [SM if a.dtype == jnp.int32 else VM for a in args]
    total = sum(a.size * a.dtype.itemsize for a in args)
    return pl.pallas_call(
        body,
        out_shape=[jax.ShapeDtypeStruct(s, t) for s, t in outs],
        in_specs=specs,
        out_specs=[VM] * len(outs),
        compiler_params=pltpu.CompilerParams(vmem_limit_bytes=40 * 2**20),
        cost_estimate=pl.CostEstimate(flops=int(flops), bytes_accessed=total, transcendentals=0),
    )(*args)


def copies(x, axis):
    count = lax.axis_size(axis)
    return lax.all_to_all(jnp.broadcast_to(x[None], (count,) + x.shape), axis, 0, 0)


def spread(x, axis):
    return copies(x.astype(jnp.float16), axis).astype(F32)


def to_heads(*arrays):
    parts = jnp.stack([a.reshape(L, 2, D).transpose(1, 0, 2) for a in arrays], axis=1)
    return lax.all_to_all(parts, "zl", 0, 0)


def to_blocks(parts):
    heads = lax.all_to_all(parts, "zl", 0, 0)
    return [heads[:, i].transpose(1, 0, 2).reshape(L, 2 * D) for i in range(heads.shape[1])]


HALF = ((D, D), F32)
PAIR = ((2, D, D), F32)
ALL = ("zl", "head")


def per_device(hidden, beta_weight, beta_bias, queries, keys, values, cotangent):
    rows, pairs = lax.axis_size("y"), lax.axis_size("zh")
    side = lax.axis_index("zl")
    at_y = lax.axis_index("y").astype(jnp.int32).reshape(1)
    at_z = lax.axis_index("zh").astype(jnp.int32).reshape(1)

    part = lax.dot_general(
        beta_weight, hidden, (((0,), (1,)), ((), ())), preferred_element_type=F32
    )
    part = part.reshape(8, 2, L).transpose(1, 0, 2).reshape(16, L)
    part = lax.all_to_all(part, ALL, 0, 0, tiled=True)
    bias = jnp.where(side == 0, beta_bias[0], beta_bias[1])
    logits = jnp.sum(part.reshape(2, 8, L), axis=1) + bias
    kv = to_heads(keys, values)
    qc = to_heads(queries, cotangent)

    send1, less, gain, inv, sk, sv, bk = call(
        kernel_prepare, [((2 * D + 16, D), F32)] + [PAIR] * 6, logits, kv
    )
    got1 = spread(send1, "zh")
    send2, own1 = call(
        functools.partial(kernel_row_forward, pairs),
        [((2 * D + 16, D), F32), ((2 * D, D), F32)], at_z, got1,
    )
    got2 = spread(send2, "y")
    (matrix,) = call(functools.partial(kernel_row_matrix, pairs), [HALF], at_z, got1)
    out, start, err, draw, back0, give, send3 = call(
        functools.partial(kernel_outputs, rows),
        [((2, L, D), BF16)] + [PAIR] * 4 + [HALF, ((D + 16, D), F32)],
        at_y, got2, own1, logits, kv, qc, less, gain, inv, sk, sv,
    )
    got3 = spread(send3, "zh")
    dq, dkp = call(
        kernel_early, [((2, L, D), BF16), PAIR], logits, kv, qc, start, err, draw
    )
    send4, own2 = call(
        functools.partial(kernel_row_back, pairs), [((D + 16, D), F32), HALF], at_z, got1, got3
    )
    got4 = spread(send4, "y")
    out, dq = to_blocks(jnp.stack([out, dq], axis=1))
    dkv, d_logits = call(
        functools.partial(kernel_grads, rows), [((2, 2, L, D), BF16), ((2, L), F32)],
        at_y, got2, got4, matrix, own2, logits, kv, less, give, start, err, back0, bk, dkp,
    )

    grads = jnp.repeat(d_logits.astype(BF16), 8, axis=0)
    grads = lax.all_to_all(grads, ALL, 0, 0, tiled=True)
    grads, dkv = lax.optimization_barrier((grads, dkv))
    all_grads = grads.reshape(2, 8, L).transpose(1, 0, 2).reshape(16, L)
    weight_part = lax.dot_general(
        all_grads, hidden, (((1,), (0,)), ((), ())), preferred_element_type=F32
    )
    bias_part = jnp.sum(d_logits)
    slot = lax.broadcasted_iota(jnp.int32, (8, 2 * D), 0) * (2 * D) + lax.broadcasted_iota(
        jnp.int32, (8, 2 * D), 1
    )
    total = jnp.concatenate([weight_part, jnp.where(slot == side, bias_part, 0.0)], axis=0)
    total = jnp.sum(copies(total, ("zh", "zl")), axis=0)
    total = jnp.sum(copies(total, "y"), axis=0)
    dk, dv = to_blocks(dkv)
    d_hidden = lax.dot_general(
        all_grads, beta_weight, (((0,), (1,)), ((), ())), preferred_element_type=F32
    )
    return (out, dq, dk, dv, d_hidden.astype(BF16), total[:16].T, total[16, 0:2])


def solution(mesh):
    grid = Mesh(mesh.devices.reshape(8, 6, 2, 8), ("y", "zh", "zl", "head"))
    seq = P(("y", "zh", "zl"), "head")
    return jax.shard_map(
        per_device,
        mesh=grid,
        in_specs=(seq, P("head", None), P("head"), seq, seq, seq, seq),
        out_specs=(seq, seq, seq, seq, seq, P("head", None), P("head")),
        check_vma=False,
    )
```

```python
import functools

import jax
import jax.numpy as jnp
from jax import lax
from jax.experimental import pallas as pl
from jax.experimental.pallas import tpu as pltpu
from jax.sharding import Mesh, PartitionSpec as P

F32 = jnp.float32
BF16 = jnp.bfloat16
L = 128
D = 128
NN = (((1,), (0,)), ((), ()))
NT = (((1,), (1,)), ((), ()))
TN = (((0,), (0,)), ((), ()))


def dot1(a, b, dims=NN):
    return lax.dot_general(a, b, dims, preferred_element_type=F32)


def split(x):
    hi = x.astype(BF16)
    return hi, (x - hi.astype(F32)).astype(BF16)


def dot2(a, b, dims=NN):
    hi, lo = split(a)
    return dot1(hi, b, dims) + dot1(lo, b, dims)


def dot2r(a, b, dims=NN):
    hi, lo = split(b)
    return dot1(a, hi, dims) + dot1(a, lo, dims)


def dot3(a, b, dims=NN):
    ah, al = split(a)
    bh, bl = split(b)
    return dot1(ah, bh, dims) + (dot1(al, bh, dims) + dot1(ah, bl, dims))


def index_grids():
    row = lax.broadcasted_iota(jnp.int32, (L, L), 0)
    col = lax.broadcasted_iota(jnp.int32, (L, L), 1)
    return row, col


def to_col(row_vec, row, col):
    return jnp.sum(jnp.where(row == col, row_vec, 0.0), axis=1, keepdims=True)


def to_row(col_vec, row, col):
    return jnp.sum(jnp.where(row == col, col_vec, 0.0), axis=0, keepdims=True)


def inv_norm(raw):
    f = raw.astype(F32)
    return lax.rsqrt(jnp.sum(f * f, axis=1, keepdims=True) + 1e-06)


def triangle_inverse(strict, row, col):
    eye = jnp.where(row == col, 1.0, 0.0)
    diff = row ^ col
    inv = eye - jnp.where(diff == 1, strict, 0.0)
    size = 2
    while size < L:
        below = jnp.where((diff >= size) & (diff < 2 * size), strict, 0.0)
        inv = inv - dot3(inv, dot3(below, inv))
        size *= 2
    return inv


def block_prepare(kr, vr, logit_row):
    row, col = index_grids()
    beta_row = 2.0 * jax.nn.sigmoid(logit_row)
    beta = to_col(beta_row, row, col)
    rk = inv_norm(kr)
    rk_row = to_row(rk, row, col)
    gram = dot1(kr, kr, NT) * rk * rk_row
    strict = jnp.where(row > col, gram * beta_row, 0.0)
    inv = triangle_inverse(strict, row, col)
    solved_k = dot2(inv * rk_row, kr)
    solved_v = dot2(inv, vr)
    scale = beta * rk
    less = dot2(solved_k * scale, kr, TN)
    gain = dot2(solved_v * scale, kr, TN)
    back_k = dot3(inv, beta * (kr.astype(F32) * rk), TN)
    return less, gain, inv, solved_k, solved_v, back_k, gram


def block_outputs(qr, kr, ct, logit_row, start, inv, solved_k, solved_v):
    row, col = index_grids()
    beta = to_col(2.0 * jax.nn.sigmoid(logit_row), row, col)
    rk, rq = inv_norm(kr), inv_norm(qr)
    rk_row = to_row(rk, row, col)
    attend = jnp.where(row >= col, dot1(qr, kr, NT) * rq * rk_row, 0.0)
    errors = solved_v - dot3(solved_k, start, NT)
    scaled = beta * errors
    raw = rq * dot2r(qr, start, NT) + dot3(attend, scaled)
    rn = lax.rsqrt(jnp.mean(raw * raw, axis=1, keepdims=True) + 1e-05)
    normed = raw * rn
    cotan = ct.astype(F32)
    d_raw = rn * (cotan - normed * jnp.mean(normed * cotan, axis=1, keepdims=True))
    back0 = dot3(inv, beta * dot3(attend, d_raw, TN), TN)
    give = dot2(d_raw * rq, qr, TN) - dot2(back0 * rk, kr, TN)
    return normed, errors, d_raw, back0, give


def block_grads_early(qr, kr, logit_row, start, errors, d_raw):
    row, col = index_grids()
    beta = to_col(2.0 * jax.nn.sigmoid(logit_row), row, col)
    rk, rq = inv_norm(kr), inv_norm(qr)
    rk_row = to_row(rk, row, col)
    scaled = beta * errors
    d_attend = jnp.where(row >= col, dot3(d_raw, scaled, NT), 0.0)
    dq_unit = dot3(d_raw, start) + dot2(d_attend * rk_row, kr)
    dk_part = dot2(d_attend * rq, qr, TN)
    q_unit = qr.astype(F32) * rq
    dq = rq * (dq_unit - q_unit * jnp.sum(q_unit * dq_unit, axis=1, keepdims=True))
    return dq, dk_part


def block_grads(kr, logit_row, start, end_grad, errors, back0, back_k, dk_part):
    row, col = index_grids()
    beta = to_col(2.0 * jax.nn.sigmoid(logit_row), row, col)
    keep = to_col(jax.nn.sigmoid(-logit_row), row, col)
    rk = inv_norm(kr)
    rk_row = to_row(rk, row, col)
    scaled = beta * errors
    back = back0 + dot3(back_k, end_grad, NT)
    d_logit = to_row(jnp.sum(errors * back, axis=1, keepdims=True) * keep, row, col)
    d_gram = jnp.where(row > col, -dot3(back, scaled, NT), 0.0)
    d_gram = d_gram + jnp.where(row < col, -dot3(scaled, back, NT), 0.0)
    dk_unit = dk_part - dot3(back, start) + dot3(scaled, end_grad) + dot2(d_gram * rk_row, kr)
    k_unit = kr.astype(F32) * rk
    dk = rk * (dk_unit - k_unit * jnp.sum(k_unit * dk_unit, axis=1, keepdims=True))
    return dk, back, d_logit


def level_of(x):
    top = jnp.max(jnp.max(jnp.abs(x), axis=1, keepdims=True), axis=0, keepdims=True)
    return jnp.ceil(jnp.log2(jnp.maximum(top, 1e-30)))


def packed(x):
    level = level_of(x)
    return x * jnp.exp2(-level), jnp.broadcast_to(level, (16, D))


def scaled_back(x, level):
    return x * jnp.exp2(level[0:1])


def step(state, less, dims=NN):
    return state - dot3(state, less, dims)


def chain_forward(less, gain, place, count):
    eye = jnp.where(index_grids()[0] == index_grids()[1], 1.0, 0.0)
    zero = jnp.zeros((D, D), F32)
    state = jnp.concatenate([eye, zero], axis=0)
    own = state
    for j in range(count):
        own = jnp.where(place == j, state, own)
        if j == 0:
            state = jnp.concatenate([eye - less(j), gain(j)], axis=0)
        else:
            state = step(state, less(j)) + jnp.concatenate([zero, gain(j)], axis=0)
    return state, own


def chain_state(less, gain, place, count):
    state = jnp.zeros((D, D), F32)
    own = state
    for j in range(count - 1):
        state = gain(j) if j == 0 else step(state, less(j)) + gain(j)
        own = jnp.where(place == j + 1, state, own)
    return own


def chain_back_matrix(less, place, count):
    state = jnp.where(index_grids()[0] == index_grids()[1], 1.0, 0.0)
    own = state
    for j in range(count - 1, 0, -1):
        state = step(state, less(j), NT)
        own = jnp.where(place == j - 1, state, own)
    return own


def chain_back(less, give, place, count, total=True):
    state = jnp.zeros((D, D), F32)
    own = state
    for j in range(count - 1, -1 if total else 0, -1):
        own = jnp.where(place == j, state, own)
        state = give(j) if j == count - 1 else step(state, less(j), NT) + give(j)
    if not total:
        own = jnp.where(place == 0, state, own)
    return state, own


def put(send, less, gain):
    send[0:D] = less
    send[D : 2 * D], send[2 * D : 2 * D + 16] = packed(gain)


def less_of(got):
    return lambda j: got[j, 0:D]


def gain_of(got):
    return lambda j: scaled_back(got[j, D : 2 * D], got[j, 2 * D : 2 * D + 8])


def give_of(got):
    return lambda j: scaled_back(got[j, 0:D], got[j, D : D + 8])


def in_order(side, mine, theirs):
    first = side[0] == 0
    return jnp.where(first, mine, theirs), jnp.where(first, theirs, mine)


def blocks_of(side, own, swapped):
    return in_order(side, jnp.where(side[0] == 0, own[:, :D], own[:, D:]), swapped)


def kernel_prepare(side, lg, k, v, swapped, send, less, gain, inv, sk, sv, bk):
    moves = []
    ks, vs = blocks_of(side, k[...], swapped[0]), blocks_of(side, v[...], swapped[1])
    for b in range(2):
        w, n, *rest, _ = block_prepare(ks[b], vs[b], lg[b : b + 1, :])
        less[b], gain[b] = w, n
        inv[b], sk[b], sv[b], bk[b] = rest
        moves.append((w, n))
    (w0, n0), (w1, n1) = moves
    both = step(jnp.concatenate([w0, n0], axis=0), w1)
    put(send, both[:D] + w1, both[D:] + n1)


def kernel_row_forward(count, place, got, send, own):
    state, before = chain_forward(less_of(got), gain_of(got), place[0], count)
    row, col = index_grids()
    put(send, jnp.where(row == col, 1.0, 0.0) - state[:D], state[D:])
    own[...] = before


def kernel_row_matrix(count, place, got, own):
    own[...] = chain_back_matrix(less_of(got), place[0], count)


def kernel_outputs(count, place, side, got, own, lg, k, q, ct, swapped, less, gain, inv, sk, sv,
                   out, start, err, draw, back0, give, send):
    ks, qs = blocks_of(side, k[...], swapped[0]), blocks_of(side, q[...], swapped[2])
    cs = blocks_of(side, ct[...], swapped[3])
    first = chain_state(less_of(got), gain_of(got), place[0], count)
    before = dot3(first, own[:D]) + own[D:]
    gives = []
    for b in range(2):
        if b == 1:
            before = step(before, less[0]) + gain[0]
        normed, e, dr, b0, g = block_outputs(
            qs[b], ks[b], cs[b], lg[b : b + 1, :], before, inv[b], sk[b], sv[b]
        )
        out[b] = normed.astype(BF16)
        start[b], err[b], draw[b], back0[b] = before, e, dr, b0
        gives.append(g)
    give[...] = gives[1]
    send[0:D], send[D : D + 16] = packed(step(gives[1], less[0], NT) + gives[0])


def kernel_early(side, lg, k, q, swapped, start, err, draw, out, mine, theirs, dkp):
    ks, qs = blocks_of(side, k[...], swapped[0]), blocks_of(side, q[...], swapped[2])
    dqs = []
    for b in range(2):
        dq, dkp[b] = block_grads_early(
            qs[b], ks[b], lg[b : b + 1, :], start[b], err[b], draw[b]
        )
        dqs.append(dq)
    mine[0], theirs[0] = in_order(side, out[0], out[1])
    dqs = in_order(side, *dqs)
    mine[1], theirs[1] = dqs[0].astype(BF16), dqs[1].astype(BF16)


def kernel_row_back(count, place, got, gives, send, own):
    state, after = chain_back(less_of(got), give_of(gives), place[0], count)
    send[0:D], send[D : D + 16] = packed(state)
    own[...] = after


def kernel_grads(count, place, side, got, gives, matrix, own, lg, k, swapped, less, give, start,
                 err, back0, bk, dkp, mine, theirs, rows, bias):
    ks = blocks_of(side, k[...], swapped[0])
    _, row_after = chain_back(less_of(got), give_of(gives), place[0], count, total=False)
    end_grad = dot3(row_after, matrix[...]) + own[...]
    later = block_grads(
        ks[1], lg[1:2, :], start[1], end_grad, err[1], back0[1], bk[1], dkp[1]
    )
    end_grad = step(end_grad, less[1], NT) + give[...]
    earlier = block_grads(
        ks[0], lg[0:1, :], start[0], end_grad, err[0], back0[0], bk[0], dkp[0]
    )
    for i in range(2):
        x, y = in_order(side, earlier[i], later[i])
        mine[i], theirs[i] = x.astype(BF16), y.astype(BF16)
    odd = lax.broadcasted_iota(jnp.int32, (16, L), 0) % 2
    rows[...] = jnp.where(odd == 0, earlier[2], later[2]).astype(BF16)
    part = jnp.sum(earlier[2] + later[2], axis=1, keepdims=True)
    row = lax.broadcasted_iota(jnp.int32, (8, 2 * D), 0)
    col = lax.broadcasted_iota(jnp.int32, (8, 2 * D), 1)
    bias[...] = jnp.where((row == 0) & (col == side[0]), part, 0.0)


VM = pl.BlockSpec(memory_space=pltpu.VMEM)
SM = pl.BlockSpec(memory_space=pltpu.SMEM)


def call(body, outs, *args, flops=1e8):
    specs = [SM if a.dtype == jnp.int32 else VM for a in args]
    total = sum(a.size * a.dtype.itemsize for a in args)
    return pl.pallas_call(
        body,
        out_shape=[jax.ShapeDtypeStruct(s, t) for s, t in outs],
        in_specs=specs,
        out_specs=[VM] * len(outs),
        compiler_params=pltpu.CompilerParams(vmem_limit_bytes=40 * 2**20),
        cost_estimate=pl.CostEstimate(flops=int(flops), bytes_accessed=total, transcendentals=0),
    )(*args)


def copies(x, axis):
    count = lax.axis_size(axis)
    return lax.all_to_all(jnp.broadcast_to(x[None], (count,) + x.shape), axis, 0, 0)


def spread(x, axis):
    return copies(x.astype(jnp.float16), axis).astype(F32)


def swap(x):
    return lax.ppermute(x, "zl", [(0, 1), (1, 0)])


def joined(side, mine, theirs):
    return jnp.where(
        side == 0,
        jnp.concatenate([mine, theirs], axis=1),
        jnp.concatenate([theirs, mine], axis=1),
    )


HALF = ((D, D), F32)
PAIR = ((2, D, D), F32)
PAIRB = ((2, L, D), BF16)
ALL = ("head", "zl")


def per_device(hidden, beta_weight, beta_bias, queries, keys, values, cotangent):
    rows, pairs = lax.axis_size("y"), lax.axis_size("zh")
    side = lax.axis_index("zl").astype(jnp.int32)
    at_y = lax.axis_index("y").astype(jnp.int32).reshape(1)
    at_z = lax.axis_index("zh").astype(jnp.int32).reshape(1)
    at_s = side.reshape(1)

    swapped = swap(
        jnp.stack([
            jnp.where(side == 0, a[:, D:], a[:, :D])
            for a in (keys, values, queries, cotangent)
        ])
    )
    part = lax.dot_general(
        beta_weight, hidden, (((0,), (1,)), ((), ())), preferred_element_type=F32
    )
    part = lax.all_to_all(part, ALL, 0, 0, tiled=True)
    bias = jnp.where(side == 0, beta_bias[0], beta_bias[1])
    logits = jnp.sum(part.reshape(8, 2, L), axis=0) + bias

    send1, less, gain, inv, sk, sv, bk = call(
        kernel_prepare, [((2 * D + 16, D), F32)] + [PAIR] * 6,
        at_s, logits, keys, values, swapped,
    )
    got1 = spread(send1, "zh")
    send2, own1 = call(
        functools.partial(kernel_row_forward, pairs),
        [((2 * D + 16, D), F32), ((2 * D, D), F32)], at_z, got1,
    )
    got2 = spread(send2, "y")
    (matrix,) = call(functools.partial(kernel_row_matrix, pairs), [HALF], at_z, got1)
    out, start, err, draw, back0, give, send3 = call(
        functools.partial(kernel_outputs, rows),
        [PAIRB] + [PAIR] * 4 + [HALF, ((D + 16, D), F32)],
        at_y, at_s, got2, own1, logits, keys, queries, cotangent, swapped,
        less, gain, inv, sk, sv,
    )
    got3 = spread(send3, "zh")
    mine, theirs, dkp = call(
        kernel_early, [PAIRB, PAIRB, PAIR],
        at_s, logits, keys, queries, swapped, start, err, draw, out,
    )
    send4, own2 = call(
        functools.partial(kernel_row_back, pairs), [((D + 16, D), F32), HALF], at_z, got1, got3
    )
    got4 = spread(send4, "y")
    theirs = swap(theirs)
    mine_kv, theirs_kv, grad_rows, bias_part = call(
        functools.partial(kernel_grads, rows),
        [PAIRB, PAIRB, ((16, L), BF16), ((8, 2 * D), F32)],
        at_y, at_s, got2, got4, matrix, own2, logits, keys, swapped, less, give, start, err,
        back0, bk, dkp,
    )

    all_grads = lax.all_to_all(grad_rows, ALL, 0, 0, tiled=True)
    all_grads, theirs_kv = lax.optimization_barrier((all_grads, theirs_kv))
    weight_part = lax.dot_general(
        all_grads, hidden, (((1,), (0,)), ((), ())), preferred_element_type=F32
    )
    total = jnp.concatenate([weight_part, bias_part], axis=0)
    total = jnp.sum(copies(total, ("zh", "zl")), axis=0)
    total = jnp.sum(copies(total, "y"), axis=0)
    theirs_kv = swap(theirs_kv)
    d_hidden = lax.dot_general(
        all_grads, beta_weight, (((0,), (1,)), ((), ())), preferred_element_type=F32
    )
    out, dq = [joined(side, mine[i], theirs[i]) for i in range(2)]
    dk, dv = [joined(side, mine_kv[i], theirs_kv[i]) for i in range(2)]
    return (out, dq, dk, dv, d_hidden.astype(BF16), total[:16].T, total[16, 0:2])


def solution(mesh):
    grid = Mesh(mesh.devices.reshape(8, 6, 2, 8), ("y", "zh", "zl", "head"))
    seq = P(("y", "zh", "zl"), "head")
    return jax.shard_map(
        per_device,
        mesh=grid,
        in_specs=(seq, P("head", None), P("head"), seq, seq, seq, seq),
        out_specs=(seq, seq, seq, seq, seq, P("head", None), P("head")),
        check_vma=False,
    )
```

```python
import functools

import jax
import jax.numpy as jnp
from jax import lax
from jax.experimental import pallas as pl
from jax.experimental.pallas import tpu as pltpu
from jax.sharding import Mesh, PartitionSpec as P

F32 = jnp.float32
BF16 = jnp.bfloat16
L = 128
D = 128
NN = (((1,), (0,)), ((), ()))
NT = (((1,), (1,)), ((), ()))
TN = (((0,), (0,)), ((), ()))


def dot1(a, b, dims=NN):
    return lax.dot_general(a, b, dims, preferred_element_type=F32)


def split(x):
    hi = x.astype(BF16)
    return hi, (x - hi.astype(F32)).astype(BF16)


def dot2(a, b, dims=NN):
    hi, lo = split(a)
    return dot1(hi, b, dims) + dot1(lo, b, dims)


def dot2r(a, b, dims=NN):
    hi, lo = split(b)
    return dot1(a, hi, dims) + dot1(a, lo, dims)


def dot3(a, b, dims=NN):
    ah, al = split(a)
    bh, bl = split(b)
    return dot1(ah, bh, dims) + (dot1(al, bh, dims) + dot1(ah, bl, dims))


def index_grids():
    row = lax.broadcasted_iota(jnp.int32, (L, L), 0)
    col = lax.broadcasted_iota(jnp.int32, (L, L), 1)
    return row, col


def to_col(row_vec, row, col):
    return jnp.sum(jnp.where(row == col, row_vec, 0.0), axis=1, keepdims=True)


def to_row(col_vec, row, col):
    return jnp.sum(jnp.where(row == col, col_vec, 0.0), axis=0, keepdims=True)


def inv_norm(raw):
    f = raw.astype(F32)
    return lax.rsqrt(jnp.sum(f * f, axis=1, keepdims=True) + 1e-06)


def triangle_inverse(strict, row, col):
    eye = jnp.where(row == col, 1.0, 0.0)
    diff = row ^ col
    inv = eye - jnp.where(diff == 1, strict, 0.0)
    size = 2
    while size < L:
        below = jnp.where((diff >= size) & (diff < 2 * size), strict, 0.0)
        inv = inv - dot3(inv, dot3(below, inv))
        size *= 2
    return inv


def block_prepare(kr, vr, logit_row):
    row, col = index_grids()
    beta_row = 2.0 * jax.nn.sigmoid(logit_row)
    beta = to_col(beta_row, row, col)
    rk = inv_norm(kr)
    rk_row = to_row(rk, row, col)
    gram = dot1(kr, kr, NT) * rk * rk_row
    strict = jnp.where(row > col, gram * beta_row, 0.0)
    inv = triangle_inverse(strict, row, col)
    solved_k = dot2(inv * rk_row, kr)
    solved_v = dot2(inv, vr)
    scale = beta * rk
    less = dot2(solved_k * scale, kr, TN)
    gain = dot2(solved_v * scale, kr, TN)
    back_k = dot3(inv, beta * (kr.astype(F32) * rk), TN)
    return less, gain, inv, solved_k, solved_v, back_k, gram


def block_outputs(qr, kr, ct, logit_row, start, inv, solved_k, solved_v):
    row, col = index_grids()
    beta = to_col(2.0 * jax.nn.sigmoid(logit_row), row, col)
    rk, rq = inv_norm(kr), inv_norm(qr)
    rk_row = to_row(rk, row, col)
    attend = jnp.where(row >= col, dot1(qr, kr, NT) * rq * rk_row, 0.0)
    errors = solved_v - dot3(solved_k, start, NT)
    scaled = beta * errors
    raw = rq * dot2r(qr, start, NT) + dot3(attend, scaled)
    rn = lax.rsqrt(jnp.mean(raw * raw, axis=1, keepdims=True) + 1e-05)
    normed = raw * rn
    cotan = ct.astype(F32)
    d_raw = rn * (cotan - normed * jnp.mean(normed * cotan, axis=1, keepdims=True))
    back0 = dot3(inv, beta * dot3(attend, d_raw, TN), TN)
    give = dot2(d_raw * rq, qr, TN) - dot2(back0 * rk, kr, TN)
    return normed, errors, d_raw, back0, give


def block_grads_early(qr, kr, logit_row, start, errors, d_raw):
    row, col = index_grids()
    beta = to_col(2.0 * jax.nn.sigmoid(logit_row), row, col)
    rk, rq = inv_norm(kr), inv_norm(qr)
    rk_row = to_row(rk, row, col)
    scaled = beta * errors
    d_attend = jnp.where(row >= col, dot3(d_raw, scaled, NT), 0.0)
    dq_unit = dot3(d_raw, start) + dot2(d_attend * rk_row, kr)
    dk_part = dot2(d_attend * rq, qr, TN)
    q_unit = qr.astype(F32) * rq
    dq = rq * (dq_unit - q_unit * jnp.sum(q_unit * dq_unit, axis=1, keepdims=True))
    return dq, dk_part


def block_grads(kr, logit_row, start, end_grad, errors, back0, back_k, dk_part):
    row, col = index_grids()
    beta = to_col(2.0 * jax.nn.sigmoid(logit_row), row, col)
    keep = to_col(jax.nn.sigmoid(-logit_row), row, col)
    rk = inv_norm(kr)
    rk_row = to_row(rk, row, col)
    scaled = beta * errors
    back = back0 + dot3(back_k, end_grad, NT)
    d_logit = to_row(jnp.sum(errors * back, axis=1, keepdims=True) * keep, row, col)
    d_gram = jnp.where(row > col, -dot3(back, scaled, NT), 0.0)
    d_gram = d_gram + jnp.where(row < col, -dot3(scaled, back, NT), 0.0)
    dk_unit = dk_part - dot3(back, start) + dot3(scaled, end_grad) + dot2(d_gram * rk_row, kr)
    k_unit = kr.astype(F32) * rk
    dk = rk * (dk_unit - k_unit * jnp.sum(k_unit * dk_unit, axis=1, keepdims=True))
    return dk, back, d_logit


def level_of(x):
    top = jnp.max(jnp.max(jnp.abs(x), axis=1, keepdims=True), axis=0, keepdims=True)
    return jnp.ceil(jnp.log2(jnp.maximum(top, 1e-30)))


def packed(x):
    level = level_of(x)
    return x * jnp.exp2(-level), jnp.broadcast_to(level, (16, D))


def scaled_back(x, level):
    return x * jnp.exp2(level[0:1])


def step(state, less, dims=NN):
    return state - dot3(state, less, dims)


def chain_forward(less, gain, place, count):
    eye = jnp.where(index_grids()[0] == index_grids()[1], 1.0, 0.0)
    zero = jnp.zeros((D, D), F32)
    state = jnp.concatenate([eye, zero], axis=0)
    own = state
    for j in range(count):
        own = jnp.where(place == j, state, own)
        if j == 0:
            state = jnp.concatenate([eye - less(j), gain(j)], axis=0)
        else:
            state = step(state, less(j)) + jnp.concatenate([zero, gain(j)], axis=0)
    return state, own


def chain_state(less, gain, place, count):
    state = jnp.zeros((D, D), F32)
    own = state
    for j in range(count - 1):
        state = gain(j) if j == 0 else step(state, less(j)) + gain(j)
        own = jnp.where(place == j + 1, state, own)
    return own


def chain_back_matrix(less, place, count):
    state = jnp.where(index_grids()[0] == index_grids()[1], 1.0, 0.0)
    own = state
    for j in range(count - 1, 0, -1):
        state = step(state, less(j), NT)
        own = jnp.where(place == j - 1, state, own)
    return own


def chain_back(less, give, place, count, total=True):
    state = jnp.zeros((D, D), F32)
    own = state
    for j in range(count - 1, -1 if total else 0, -1):
        own = jnp.where(place == j, state, own)
        state = give(j) if j == count - 1 else step(state, less(j), NT) + give(j)
    if not total:
        own = jnp.where(place == 0, state, own)
    return state, own


def put(send, less, gain):
    send[0:D] = less
    send[D : 2 * D], send[2 * D : 2 * D + 16] = packed(gain)


def less_of(got):
    return lambda j: got[j, 0:D]


def gain_of(got):
    return lambda j: scaled_back(got[j, D : 2 * D], got[j, 2 * D : 2 * D + 8])


def give_of(got):
    return lambda j: scaled_back(got[j, 0:D], got[j, D : D + 8])


def in_order(side, mine, theirs):
    first = side[0] == 0
    return jnp.where(first, mine, theirs), jnp.where(first, theirs, mine)


def kernel_first(side, slot, bias, weight, hidden, k, v, q, ct, part, mine, theirs,
                 offset, narrow, held, done):
    small = pltpu.make_async_copy(bias, offset, done.at[6])
    small.start()
    copies = [pltpu.make_async_copy(weight, narrow, done.at[5])] + [
        pltpu.make_async_copy(x, held.at[i], done.at[i])
        for i, x in enumerate((hidden, k, v, q, ct))
    ]
    for copy in copies:
        copy.start()
    copies[0].wait()
    copies[1].wait()
    small.wait()
    head = lax.broadcasted_iota(jnp.int32, (16, L), 0) - 2 * slot[0]
    own = jnp.where(head == 0, offset[0], jnp.where(head == 1, offset[1], 0.0))
    part[...] = dot1(narrow[...], held[0], NT) + own
    for i in range(4):
        copies[i + 2].wait()
        mine[i], theirs[i] = in_order(side, held[i + 1, :, :D], held[i + 1, :, D:])


def kernel_prepare(side, part, mine, swapped, send, lg, less, gain, inv, sk, sv, bk):
    odd = lax.broadcasted_iota(jnp.int32, (16, L), 0) % 2
    moves = []
    ks, vs = in_order(side, mine[0], swapped[0]), in_order(side, mine[1], swapped[1])
    for b in range(2):
        logit = jnp.sum(jnp.where(odd == b, part[...], 0.0), axis=0, keepdims=True)
        lg[b : b + 1, :] = logit
        w, n, *rest, _ = block_prepare(ks[b], vs[b], logit)
        less[b], gain[b] = w, n
        inv[b], sk[b], sv[b], bk[b] = rest
        moves.append((w, n))
    (w0, n0), (w1, n1) = moves
    both = step(jnp.concatenate([w0, n0], axis=0), w1)
    put(send, both[:D] + w1, both[D:] + n1)


def kernel_row_forward(count, place, got, send, own):
    state, before = chain_forward(less_of(got), gain_of(got), place[0], count)
    row, col = index_grids()
    put(send, jnp.where(row == col, 1.0, 0.0) - state[:D], state[D:])
    own[...] = before


def kernel_row_matrix(count, place, got, own):
    own[...] = chain_back_matrix(less_of(got), place[0], count)


def kernel_outputs(count, place, side, got, own, lg, mine, swapped, less, gain, inv, sk, sv,
                   out, start, err, draw, back0, give, send):
    ks, qs = in_order(side, mine[0], swapped[0]), in_order(side, mine[2], swapped[2])
    cs = in_order(side, mine[3], swapped[3])
    first = chain_state(less_of(got), gain_of(got), place[0], count)
    before = dot3(first, own[:D]) + own[D:]
    gives = []
    for b in range(2):
        if b == 1:
            before = step(before, less[0]) + gain[0]
        normed, e, dr, b0, g = block_outputs(
            qs[b], ks[b], cs[b], lg[b : b + 1, :], before, inv[b], sk[b], sv[b]
        )
        out[b] = normed.astype(BF16)
        start[b], err[b], draw[b], back0[b] = before, e, dr, b0
        gives.append(g)
    give[...] = gives[1]
    send[0:D], send[D : D + 16] = packed(step(gives[1], less[0], NT) + gives[0])


def kernel_early(side, lg, own, swapped, start, err, draw, out, mine, theirs, dkp):
    ks, qs = in_order(side, own[0], swapped[0]), in_order(side, own[2], swapped[2])
    dqs = []
    for b in range(2):
        dq, dkp[b] = block_grads_early(
            qs[b], ks[b], lg[b : b + 1, :], start[b], err[b], draw[b]
        )
        dqs.append(dq)
    mine[0], theirs[0] = in_order(side, out[0], out[1])
    dqs = in_order(side, *dqs)
    mine[1], theirs[1] = dqs[0].astype(BF16), dqs[1].astype(BF16)


def kernel_row_back(count, place, got, gives, send, own):
    state, after = chain_back(less_of(got), give_of(gives), place[0], count)
    send[0:D], send[D : D + 16] = packed(state)
    own[...] = after


def kernel_grads(count, place, side, got, gives, matrix, own, lg, held, swapped, less, give,
                 start, err, back0, bk, dkp, mine, theirs, message):
    ks = in_order(side, held[0], swapped[0])
    _, row_after = chain_back(less_of(got), give_of(gives), place[0], count, total=False)
    end_grad = dot3(row_after, matrix[...]) + own[...]
    later = block_grads(
        ks[1], lg[1:2, :], start[1], end_grad, err[1], back0[1], bk[1], dkp[1]
    )
    end_grad = step(end_grad, less[1], NT) + give[...]
    earlier = block_grads(
        ks[0], lg[0:1, :], start[0], end_grad, err[0], back0[0], bk[0], dkp[0]
    )
    for i in range(2):
        x, y = in_order(side, earlier[i], later[i])
        mine[i], theirs[i] = x.astype(BF16), y.astype(BF16)
    odd = lax.broadcasted_iota(jnp.int32, (192, L), 0) % 2
    message[...] = jnp.where(odd == 0, earlier[2], later[2])


def kernel_weight(pairs, place, side, slot, got, hidden, total, grads, held, done):
    copies = [
        pltpu.make_async_copy(hidden.at[pl.ds(2 * j, 2)], held.at[pl.ds(2 * j, 2)], done.at[j])
        for j in range(pairs)
    ]
    for copy in copies:
        copy.start()
    weight = jnp.zeros((16, 2 * D), F32)
    bias = jnp.zeros((16, 1), F32)
    for j in range(pairs):
        copies[j].wait()
        for b in range(2):
            rows = got[pl.ds(32 * j + b, 16, stride=2), :]
            weight = weight + dot1(rows.astype(BF16), held[2 * j + b].astype(BF16))
            bias = bias + jnp.sum(rows, axis=1, keepdims=True)
    row = lax.broadcasted_iota(jnp.int32, (16, 2 * D), 0)
    col = lax.broadcasted_iota(jnp.int32, (16, 2 * D), 1)
    line = jnp.sum(
        jnp.where((row - 2 * slot[0] == col) & (col < 2), bias, 0.0), axis=0, keepdims=True
    )
    for i in range(total.shape[0]):
        total[i, 0:16] = weight
        total[i, 16:24] = jnp.broadcast_to(line, (8, 2 * D))
    here = [got[pl.ds(32 * place[0] + b, 16, stride=2), :] for b in range(2)]
    grads[...] = in_order(side, *here)[0].astype(BF16)


VM = pl.BlockSpec(memory_space=pltpu.VMEM)
SM = pl.BlockSpec(memory_space=pltpu.SMEM)


def call(body, outs, *args, flops=1e8):
    specs = [SM if a.ndim == 1 else VM for a in args]
    total = sum(a.size * a.dtype.itemsize for a in args)
    return pl.pallas_call(
        body,
        out_shape=[jax.ShapeDtypeStruct(s, t) for s, t in outs],
        in_specs=specs,
        out_specs=[VM] * len(outs),
        compiler_params=pltpu.CompilerParams(vmem_limit_bytes=16 * 2**20),
        cost_estimate=pl.CostEstimate(flops=int(flops), bytes_accessed=total, transcendentals=0),
    )(*args)


def copies(x, axis):
    count = lax.axis_size(axis)
    return lax.all_to_all(jnp.broadcast_to(x[None], (count,) + x.shape), axis, 0, 0)


def spread(x, axis):
    return copies(x.astype(jnp.float16), axis).astype(F32)


def swap(x):
    return lax.ppermute(x, "zl", [(0, 1), (1, 0)])


def joined(side, mine, theirs):
    return jnp.where(
        side == 0,
        jnp.concatenate([mine, theirs], axis=1),
        jnp.concatenate([theirs, mine], axis=1),
    )


HALF = ((D, D), F32)
PAIR = ((2, D, D), F32)
PAIRB = ((2, L, D), BF16)


def per_device(hidden, beta_weight, beta_bias, queries, keys, values, cotangent):
    rows, pairs = lax.axis_size("y"), lax.axis_size("zh")
    side = lax.axis_index("zl").astype(jnp.int32)
    at_y = lax.axis_index("y").astype(jnp.int32).reshape(1)
    at_z = lax.axis_index("zh").astype(jnp.int32).reshape(1)
    at_s = side.reshape(1)

    at_h = lax.axis_index("head").astype(jnp.int32).reshape(1)

    four = jax.ShapeDtypeStruct((4, L, D), BF16)
    part, held, theirs = pl.pallas_call(
        kernel_first,
        out_shape=[jax.ShapeDtypeStruct((16, L), F32), four, four],
        in_specs=[SM] * 2 + [pl.BlockSpec(memory_space=pl.ANY)] * 7,
        out_specs=[VM] * 3,
        scratch_shapes=[
            pltpu.SMEM((2,), F32),
            pltpu.VMEM((16, 2 * D), BF16),
            pltpu.VMEM((5, L, 2 * D), BF16),
            pltpu.SemaphoreType.DMA((7,)),
        ],
        compiler_params=pltpu.CompilerParams(vmem_limit_bytes=60 * 2**20),
        cost_estimate=pl.CostEstimate(flops=10**7, bytes_accessed=10**6, transcendentals=0),
    )(at_s, at_h, beta_bias, beta_weight.T, hidden, keys, values, queries, cotangent)
    part = lax.all_to_all(part, ("head", "zl"), 0, 0, tiled=True)
    swapped = swap(theirs)

    send1, logits, less, gain, inv, sk, sv, bk = call(
        kernel_prepare, [((2 * D + 16, D), F32), ((2, L), F32)] + [PAIR] * 6,
        at_s, part, held, swapped,
    )
    got1 = spread(send1, "zh")
    send2, own1 = call(
        functools.partial(kernel_row_forward, pairs),
        [((2 * D + 16, D), F32), ((2 * D, D), F32)], at_z, got1,
    )
    send2, hidden_f = lax.optimization_barrier((send2, hidden))
    hidden_row = lax.all_gather(hidden_f.astype(F32), ("zh", "zl"))
    got2 = spread(send2, "y")
    (matrix,) = call(functools.partial(kernel_row_matrix, pairs), [HALF], at_z, got1)
    out, start, err, draw, back0, give, send3 = call(
        functools.partial(kernel_outputs, rows),
        [PAIRB] + [PAIR] * 4 + [HALF, ((D + 16, D), F32)],
        at_y, at_s, got2, own1, logits, held, swapped, less, gain, inv, sk, sv,
    )
    got3 = spread(send3, "zh")
    mine, theirs, dkp = call(
        kernel_early, [PAIRB, PAIRB, PAIR],
        at_s, logits, held, swapped, start, err, draw, out,
    )
    send4, own2 = call(
        functools.partial(kernel_row_back, pairs), [((D + 16, D), F32), HALF], at_z, got1, got3
    )
    got4 = spread(send4, "y")
    theirs = swap(theirs)
    mine_kv, theirs_kv, message = call(
        functools.partial(kernel_grads, rows), [PAIRB, PAIRB, ((192, L), F32)],
        at_y, at_s, got2, got4, matrix, own2, logits, held, swapped, less, give, start, err,
        back0, bk, dkp,
    )

    message = lax.all_to_all(message.reshape(96, 2, L), ("zh", "head", "zl"), 0, 0)
    message, theirs_kv = lax.optimization_barrier((message, theirs_kv))
    total, grads = pl.pallas_call(
        functools.partial(kernel_weight, pairs),
        out_shape=[
            jax.ShapeDtypeStruct((rows, 24, 2 * D), F32), jax.ShapeDtypeStruct((16, L), BF16)
        ],
        in_specs=[SM] * 3 + [VM, pl.BlockSpec(memory_space=pl.ANY)],
        out_specs=[VM] * 2,
        scratch_shapes=[
            pltpu.VMEM((2 * pairs, L, 2 * D), F32), pltpu.SemaphoreType.DMA((pairs,))
        ],
        compiler_params=pltpu.CompilerParams(vmem_limit_bytes=60 * 2**20),
        cost_estimate=pl.CostEstimate(flops=10**8, bytes_accessed=10**6, transcendentals=0),
    )(at_z, at_s, at_h, message.reshape(192, L), hidden_row)
    total = jnp.sum(lax.all_to_all(total, "y", 0, 0), axis=0)
    theirs_kv = swap(theirs_kv)
    d_hidden = lax.dot_general(
        grads, beta_weight, (((0,), (1,)), ((), ())), preferred_element_type=F32
    )
    out, dq = [joined(side, mine[i], theirs[i]) for i in range(2)]
    dk, dv = [joined(side, mine_kv[i], theirs_kv[i]) for i in range(2)]
    return (out, dq, dk, dv, d_hidden.astype(BF16), total[:16].T, total[16, 0:2])


def solution(mesh):
    grid = Mesh(mesh.devices.reshape(8, 6, 2, 8), ("y", "zh", "zl", "head"))
    seq = P(("y", "zh", "zl"), "head")
    return jax.shard_map(
        per_device,
        mesh=grid,
        in_specs=(seq, P("head", None), P("head"), seq, seq, seq, seq),
        out_specs=(seq, seq, seq, seq, seq, P("head", None), P("head")),
        check_vma=False,
    )
```

```python
import functools

import jax
import jax.numpy as jnp
from jax import lax
from jax.experimental import pallas as pl
from jax.experimental.pallas import tpu as pltpu
from jax.sharding import Mesh, PartitionSpec as P

F32 = jnp.float32
BF16 = jnp.bfloat16
L = 128
D = 128
NN = (((1,), (0,)), ((), ()))
NT = (((1,), (1,)), ((), ()))
TN = (((0,), (0,)), ((), ()))


def dot1(a, b, dims=NN):
    return lax.dot_general(a, b, dims, preferred_element_type=F32)


def split(x):
    hi = x.astype(BF16)
    return hi, (x - hi.astype(F32)).astype(BF16)


def dot2(a, b, dims=NN):
    hi, lo = split(a)
    return dot1(hi, b, dims) + dot1(lo, b, dims)


def dot2r(a, b, dims=NN):
    hi, lo = split(b)
    return dot1(a, hi, dims) + dot1(a, lo, dims)


def dot3(a, b, dims=NN):
    ah, al = split(a)
    bh, bl = split(b)
    return dot1(ah, bh, dims) + (dot1(al, bh, dims) + dot1(ah, bl, dims))


def index_grids():
    row = lax.broadcasted_iota(jnp.int32, (L, L), 0)
    col = lax.broadcasted_iota(jnp.int32, (L, L), 1)
    return row, col


def to_col(row_vec, row, col):
    return jnp.sum(jnp.where(row == col, row_vec, 0.0), axis=1, keepdims=True)


def to_row(col_vec, row, col):
    return jnp.sum(jnp.where(row == col, col_vec, 0.0), axis=0, keepdims=True)


def inv_norm(raw):
    f = raw.astype(F32)
    return lax.rsqrt(jnp.sum(f * f, axis=1, keepdims=True) + 1e-06)


def triangle_inverse(strict, row, col):
    eye = jnp.where(row == col, 1.0, 0.0)
    diff = row ^ col
    inv = eye - jnp.where(diff == 1, strict, 0.0)
    size = 2
    while size < L:
        below = jnp.where((diff >= size) & (diff < 2 * size), strict, 0.0)
        inv = inv - dot3(inv, dot3(below, inv))
        size *= 2
    return inv


def block_prepare(kr, vr, logit_row):
    row, col = index_grids()
    beta_row = 2.0 * jax.nn.sigmoid(logit_row)
    beta = to_col(beta_row, row, col)
    rk = inv_norm(kr)
    rk_row = to_row(rk, row, col)
    gram = dot1(kr, kr, NT) * rk * rk_row
    strict = jnp.where(row > col, gram * beta_row, 0.0)
    inv = triangle_inverse(strict, row, col)
    solved_k = dot2(inv * rk_row, kr)
    solved_v = dot2(inv, vr)
    scale = beta * rk
    less = dot2(solved_k * scale, kr, TN)
    gain = dot2(solved_v * scale, kr, TN)
    back_k = dot3(inv, beta * (kr.astype(F32) * rk), TN)
    return less, gain, inv, solved_k, solved_v, back_k, gram


def block_outputs(qr, kr, ct, logit_row, start, inv, solved_k, solved_v):
    row, col = index_grids()
    beta = to_col(2.0 * jax.nn.sigmoid(logit_row), row, col)
    rk, rq = inv_norm(kr), inv_norm(qr)
    rk_row = to_row(rk, row, col)
    attend = jnp.where(row >= col, dot1(qr, kr, NT) * rq * rk_row, 0.0)
    errors = solved_v - dot3(solved_k, start, NT)
    scaled = beta * errors
    raw = rq * dot2r(qr, start, NT) + dot3(attend, scaled)
    rn = lax.rsqrt(jnp.mean(raw * raw, axis=1, keepdims=True) + 1e-05)
    normed = raw * rn
    cotan = ct.astype(F32)
    d_raw = rn * (cotan - normed * jnp.mean(normed * cotan, axis=1, keepdims=True))
    back0 = dot3(inv, beta * dot3(attend, d_raw, TN), TN)
    give = dot2(d_raw * rq, qr, TN) - dot2(back0 * rk, kr, TN)
    return normed, errors, d_raw, back0, give


def block_grads_early(qr, kr, logit_row, start, errors, d_raw):
    row, col = index_grids()
    beta = to_col(2.0 * jax.nn.sigmoid(logit_row), row, col)
    rk, rq = inv_norm(kr), inv_norm(qr)
    rk_row = to_row(rk, row, col)
    scaled = beta * errors
    d_attend = jnp.where(row >= col, dot3(d_raw, scaled, NT), 0.0)
    dq_unit = dot3(d_raw, start) + dot2(d_attend * rk_row, kr)
    dk_part = dot2(d_attend * rq, qr, TN)
    q_unit = qr.astype(F32) * rq
    dq = rq * (dq_unit - q_unit * jnp.sum(q_unit * dq_unit, axis=1, keepdims=True))
    return dq, dk_part


def block_grads(kr, logit_row, start, end_grad, errors, back0, back_k, dk_part):
    row, col = index_grids()
    beta = to_col(2.0 * jax.nn.sigmoid(logit_row), row, col)
    keep = to_col(jax.nn.sigmoid(-logit_row), row, col)
    rk = inv_norm(kr)
    rk_row = to_row(rk, row, col)
    scaled = beta * errors
    back = back0 + dot3(back_k, end_grad, NT)
    d_logit = to_row(jnp.sum(errors * back, axis=1, keepdims=True) * keep, row, col)
    d_gram = jnp.where(row > col, -dot3(back, scaled, NT), 0.0)
    d_gram = d_gram + jnp.where(row < col, -dot3(scaled, back, NT), 0.0)
    dk_unit = dk_part - dot3(back, start) + dot3(scaled, end_grad) + dot2(d_gram * rk_row, kr)
    k_unit = kr.astype(F32) * rk
    dk = rk * (dk_unit - k_unit * jnp.sum(k_unit * dk_unit, axis=1, keepdims=True))
    return dk, back, d_logit


def level_of(x):
    top = jnp.max(jnp.max(jnp.abs(x), axis=1, keepdims=True), axis=0, keepdims=True)
    return jnp.ceil(jnp.log2(jnp.maximum(top, 1e-30)))


def packed(x):
    level = level_of(x)
    return x * jnp.exp2(-level), jnp.broadcast_to(level, (16, D))


def scaled_back(x, level):
    return x * jnp.exp2(level[0:1])


def step(state, less, dims=NN):
    return state - dot3(state, less, dims)


def chain_forward(less, gain, place, count):
    eye = jnp.where(index_grids()[0] == index_grids()[1], 1.0, 0.0)
    zero = jnp.zeros((D, D), F32)
    state = jnp.concatenate([eye, zero], axis=0)
    own = state
    for j in range(count):
        own = jnp.where(place == j, state, own)
        if j == 0:
            state = jnp.concatenate([eye - less(j), gain(j)], axis=0)
        else:
            state = step(state, less(j)) + jnp.concatenate([zero, gain(j)], axis=0)
    return state, own


def chain_state(less, gain, place, count):
    state = jnp.zeros((D, D), F32)
    own = state
    for j in range(count - 1):
        state = gain(j) if j == 0 else step(state, less(j)) + gain(j)
        own = jnp.where(place == j + 1, state, own)
    return own


def chain_back_matrix(less, place, count):
    state = jnp.where(index_grids()[0] == index_grids()[1], 1.0, 0.0)
    own = state
    for j in range(count - 1, 0, -1):
        state = step(state, less(j), NT)
        own = jnp.where(place == j - 1, state, own)
    return own


def chain_back(less, give, place, count, total=True):
    state = jnp.zeros((D, D), F32)
    own = state
    for j in range(count - 1, -1 if total else 0, -1):
        own = jnp.where(place == j, state, own)
        state = give(j) if j == count - 1 else step(state, less(j), NT) + give(j)
    if not total:
        own = jnp.where(place == 0, state, own)
    return state, own


def put(send, less, gain):
    send[0:D] = less
    send[D : 2 * D], send[2 * D : 2 * D + 16] = packed(gain)


def less_of(got):
    return lambda j: got[j, 0:D]


def gain_of(got):
    return lambda j: scaled_back(got[j, D : 2 * D], got[j, 2 * D : 2 * D + 8])


def give_of(got):
    return lambda j: scaled_back(got[j, 0:D], got[j, D : D + 8])


def in_order(side, mine, theirs):
    first = side[0] == 0
    return jnp.where(first, mine, theirs), jnp.where(first, theirs, mine)


def kernel_first(side, slot, bias, weight, hidden, k, v, q, ct, part, mine, theirs,
                 offset, narrow, held, done):
    small = pltpu.make_async_copy(bias, offset, done.at[6])
    small.start()
    copies = [pltpu.make_async_copy(weight, narrow, done.at[5])] + [
        pltpu.make_async_copy(x, held.at[i], done.at[i])
        for i, x in enumerate((hidden, k, v, q, ct))
    ]
    for copy in copies:
        copy.start()
    copies[0].wait()
    copies[1].wait()
    small.wait()
    head = lax.broadcasted_iota(jnp.int32, (16, L), 0) - 2 * slot[0]
    own = jnp.where(head == 0, offset[0], jnp.where(head == 1, offset[1], 0.0))
    part[...] = dot1(narrow[...], held[0], NT) + own
    for i in range(4):
        copies[i + 2].wait()
        mine[i], theirs[i] = in_order(side, held[i + 1, :, :D], held[i + 1, :, D:])


def kernel_prepare(side, part, mine, swapped, send, lg, less, gain, inv, sk, sv, bk):
    odd = lax.broadcasted_iota(jnp.int32, (16, L), 0) % 2
    moves = []
    ks, vs = in_order(side, mine[0], swapped[0]), in_order(side, mine[1], swapped[1])
    for b in range(2):
        logit = jnp.sum(jnp.where(odd == b, part[...], 0.0), axis=0, keepdims=True)
        lg[b : b + 1, :] = logit
        w, n, *rest, _ = block_prepare(ks[b], vs[b], logit)
        less[b], gain[b] = w, n
        inv[b], sk[b], sv[b], bk[b] = rest
        moves.append((w, n))
    (w0, n0), (w1, n1) = moves
    both = step(jnp.concatenate([w0, n0], axis=0), w1)
    put(send, both[:D] + w1, both[D:] + n1)


def kernel_row_forward(count, place, got, send, own):
    state, before = chain_forward(less_of(got), gain_of(got), place[0], count)
    row, col = index_grids()
    put(send, jnp.where(row == col, 1.0, 0.0) - state[:D], state[D:])
    own[...] = before


def kernel_row_matrix(count, place, got, own):
    own[...] = chain_back_matrix(less_of(got), place[0], count)


def kernel_outputs(count, place, side, got, own, lg, mine, swapped, less, gain, inv, sk, sv,
                   out, start, err, draw, back0, give, send):
    ks, qs = in_order(side, mine[0], swapped[0]), in_order(side, mine[2], swapped[2])
    cs = in_order(side, mine[3], swapped[3])
    first = chain_state(less_of(got), gain_of(got), place[0], count)
    before = dot3(first, own[:D]) + own[D:]
    gives = []
    for b in range(2):
        if b == 1:
            before = step(before, less[0]) + gain[0]
        normed, e, dr, b0, g = block_outputs(
            qs[b], ks[b], cs[b], lg[b : b + 1, :], before, inv[b], sk[b], sv[b]
        )
        out[b] = normed.astype(BF16)
        start[b], err[b], draw[b], back0[b] = before, e, dr, b0
        gives.append(g)
    give[...] = gives[1]
    send[0:D], send[D : D + 16] = packed(step(gives[1], less[0], NT) + gives[0])


def kernel_early(side, lg, own, swapped, start, err, draw, out, mine, theirs, dkp):
    ks, qs = in_order(side, own[0], swapped[0]), in_order(side, own[2], swapped[2])
    dqs = []
    for b in range(2):
        dq, dkp[b] = block_grads_early(
            qs[b], ks[b], lg[b : b + 1, :], start[b], err[b], draw[b]
        )
        dqs.append(dq)
    mine[0], theirs[0] = in_order(side, out[0], out[1])
    dqs = in_order(side, *dqs)
    mine[1], theirs[1] = dqs[0].astype(BF16), dqs[1].astype(BF16)


def kernel_row_back(count, place, got, gives, send, own):
    state, after = chain_back(less_of(got), give_of(gives), place[0], count)
    send[0:D], send[D : D + 16] = packed(state)
    own[...] = after


def kernel_grads(count, place, side, got, gives, matrix, own, lg, held, swapped, less, give,
                 start, err, back0, bk, dkp, mine, theirs, message):
    ks = in_order(side, held[0], swapped[0])
    _, row_after = chain_back(less_of(got), give_of(gives), place[0], count, total=False)
    end_grad = dot3(row_after, matrix[...]) + own[...]
    later = block_grads(
        ks[1], lg[1:2, :], start[1], end_grad, err[1], back0[1], bk[1], dkp[1]
    )
    end_grad = step(end_grad, less[1], NT) + give[...]
    earlier = block_grads(
        ks[0], lg[0:1, :], start[0], end_grad, err[0], back0[0], bk[0], dkp[0]
    )
    for i in range(2):
        x, y = in_order(side, earlier[i], later[i])
        mine[i], theirs[i] = x.astype(BF16), y.astype(BF16)
    odd = lax.broadcasted_iota(jnp.int32, (32, L), 0) % 2
    message[...] = jnp.where(odd == 0, earlier[2], later[2])


def kernel_weight(side, slot, got, hidden, swapped, total, grads):
    rows = [got[pl.ds(b, 16, stride=2), :] for b in range(2)]
    here, there = in_order(side, *rows)
    grads[...] = here.astype(BF16)
    weight = dot1(here.astype(BF16), hidden[...]) + dot1(there.astype(BF16), swapped[...])
    bias = jnp.sum(rows[0] + rows[1], axis=1, keepdims=True)
    row = lax.broadcasted_iota(jnp.int32, (16, 2 * D), 0)
    col = lax.broadcasted_iota(jnp.int32, (16, 2 * D), 1)
    line = jnp.sum(
        jnp.where((row - 2 * slot[0] == col) & (col < 2), bias, 0.0), axis=0, keepdims=True
    )
    for i in range(total.shape[0]):
        total[i, 0:16] = weight
        total[i, 16:24] = jnp.broadcast_to(line, (8, 2 * D))


VM = pl.BlockSpec(memory_space=pltpu.VMEM)
SM = pl.BlockSpec(memory_space=pltpu.SMEM)


def call(body, outs, *args, flops=1e8):
    specs = [SM if a.ndim == 1 else VM for a in args]
    total = sum(a.size * a.dtype.itemsize for a in args)
    return pl.pallas_call(
        body,
        out_shape=[jax.ShapeDtypeStruct(s, t) for s, t in outs],
        in_specs=specs,
        out_specs=[VM] * len(outs),
        compiler_params=pltpu.CompilerParams(vmem_limit_bytes=16 * 2**20),
        cost_estimate=pl.CostEstimate(flops=int(flops), bytes_accessed=total, transcendentals=0),
    )(*args)


def copies(x, axis):
    count = lax.axis_size(axis)
    return lax.all_to_all(jnp.broadcast_to(x[None], (count,) + x.shape), axis, 0, 0)


def spread(x, axis):
    return copies(x.astype(jnp.float16), axis).astype(F32)


def swap(x):
    return lax.ppermute(x, "zl", [(0, 1), (1, 0)])


def joined(side, mine, theirs):
    return jnp.where(
        side == 0,
        jnp.concatenate([mine, theirs], axis=1),
        jnp.concatenate([theirs, mine], axis=1),
    )


HALF = ((D, D), F32)
PAIR = ((2, D, D), F32)
PAIRB = ((2, L, D), BF16)


def per_device(hidden, beta_weight, beta_bias, queries, keys, values, cotangent):
    rows, pairs = lax.axis_size("y"), lax.axis_size("zh")
    side = lax.axis_index("zl").astype(jnp.int32)
    at_y = lax.axis_index("y").astype(jnp.int32).reshape(1)
    at_z = lax.axis_index("zh").astype(jnp.int32).reshape(1)
    at_s = side.reshape(1)

    at_h = lax.axis_index("head").astype(jnp.int32).reshape(1)

    four = jax.ShapeDtypeStruct((4, L, D), BF16)
    part, held, theirs = pl.pallas_call(
        kernel_first,
        out_shape=[jax.ShapeDtypeStruct((16, L), F32), four, four],
        in_specs=[SM] * 2 + [pl.BlockSpec(memory_space=pl.ANY)] * 7,
        out_specs=[VM] * 3,
        scratch_shapes=[
            pltpu.SMEM((2,), F32),
            pltpu.VMEM((16, 2 * D), BF16),
            pltpu.VMEM((5, L, 2 * D), BF16),
            pltpu.SemaphoreType.DMA((7,)),
        ],
        compiler_params=pltpu.CompilerParams(vmem_limit_bytes=60 * 2**20),
        cost_estimate=pl.CostEstimate(flops=10**7, bytes_accessed=10**6, transcendentals=0),
    )(at_s, at_h, beta_bias, beta_weight.T, hidden, keys, values, queries, cotangent)
    part = lax.all_to_all(part, ("head", "zl"), 0, 0, tiled=True)
    swapped = swap(theirs)

    send1, logits, less, gain, inv, sk, sv, bk = call(
        kernel_prepare, [((2 * D + 16, D), F32), ((2, L), F32)] + [PAIR] * 6,
        at_s, part, held, swapped,
    )
    got1 = spread(send1, "zh")
    send2, own1 = call(
        functools.partial(kernel_row_forward, pairs),
        [((2 * D + 16, D), F32), ((2 * D, D), F32)], at_z, got1,
    )
    send2, hidden_s = lax.optimization_barrier((send2, hidden))
    hidden_s = swap(hidden_s)
    got2, hidden_s = lax.optimization_barrier((spread(send2, "y"), hidden_s))
    (matrix,) = call(functools.partial(kernel_row_matrix, pairs), [HALF], at_z, got1)
    out, start, err, draw, back0, give, send3 = call(
        functools.partial(kernel_outputs, rows),
        [PAIRB] + [PAIR] * 4 + [HALF, ((D + 16, D), F32)],
        at_y, at_s, got2, own1, logits, held, swapped, less, gain, inv, sk, sv,
    )
    got3 = spread(send3, "zh")
    mine, theirs, dkp = call(
        kernel_early, [PAIRB, PAIRB, PAIR],
        at_s, logits, held, swapped, start, err, draw, out,
    )
    send4, own2 = call(
        functools.partial(kernel_row_back, pairs), [((D + 16, D), F32), HALF], at_z, got1, got3
    )
    got4 = spread(send4, "y")
    theirs = swap(theirs)
    mine_kv, theirs_kv, message = call(
        functools.partial(kernel_grads, rows), [PAIRB, PAIRB, ((32, L), F32)],
        at_y, at_s, got2, got4, matrix, own2, logits, held, swapped, less, give, start, err,
        back0, bk, dkp,
    )

    message = lax.all_to_all(message.reshape(16, 2, L), ("head", "zl"), 0, 0)
    total, grads = call(
        kernel_weight, [((pairs, 24, 2 * D), F32), ((16, L), BF16)],
        at_s, at_h, message.reshape(32, L), hidden, hidden_s,
    )
    total, theirs_kv = lax.optimization_barrier((total, theirs_kv))
    total = jnp.sum(lax.all_to_all(total, "zh", 0, 0), axis=0)
    total = jnp.sum(copies(total, "y"), axis=0)
    theirs_kv = swap(theirs_kv)
    d_hidden = lax.dot_general(
        grads, beta_weight, (((0,), (1,)), ((), ())), preferred_element_type=F32
    )
    out, dq = [joined(side, mine[i], theirs[i]) for i in range(2)]
    dk, dv = [joined(side, mine_kv[i], theirs_kv[i]) for i in range(2)]
    return (out, dq, dk, dv, d_hidden.astype(BF16), total[:16].T, total[16, 0:2])


def solution(mesh):
    grid = Mesh(mesh.devices.reshape(8, 6, 2, 8), ("y", "zh", "zl", "head"))
    seq = P(("y", "zh", "zl"), "head")
    return jax.shard_map(
        per_device,
        mesh=grid,
        in_specs=(seq, P("head", None), P("head"), seq, seq, seq, seq),
        out_specs=(seq, seq, seq, seq, seq, P("head", None), P("head")),
        check_vma=False,
    )
```

```python
import functools

import jax
import jax.numpy as jnp
from jax import lax
from jax.experimental import pallas as pl
from jax.experimental.pallas import tpu as pltpu
from jax.sharding import Mesh, PartitionSpec as P

F32 = jnp.float32
BF16 = jnp.bfloat16
L = 128
D = 128
NN = (((1,), (0,)), ((), ()))
NT = (((1,), (1,)), ((), ()))
TN = (((0,), (0,)), ((), ()))


def dot1(a, b, dims=NN):
    return lax.dot_general(a, b, dims, preferred_element_type=F32)


def split(x):
    hi = x.astype(BF16)
    return hi, (x - hi.astype(F32)).astype(BF16)


def dot2(a, b, dims=NN):
    hi, lo = split(a)
    return dot1(hi, b, dims) + dot1(lo, b, dims)


def dot2r(a, b, dims=NN):
    hi, lo = split(b)
    return dot1(a, hi, dims) + dot1(a, lo, dims)


def dot3(a, b, dims=NN):
    ah, al = split(a)
    bh, bl = split(b)
    return dot1(ah, bh, dims) + (dot1(al, bh, dims) + dot1(ah, bl, dims))


def index_grids():
    row = lax.broadcasted_iota(jnp.int32, (L, L), 0)
    col = lax.broadcasted_iota(jnp.int32, (L, L), 1)
    return row, col


def to_col(row_vec, row, col):
    return jnp.sum(jnp.where(row == col, row_vec, 0.0), axis=1, keepdims=True)


def to_row(col_vec, row, col):
    return jnp.sum(jnp.where(row == col, col_vec, 0.0), axis=0, keepdims=True)


def inv_norm(raw):
    f = raw.astype(F32)
    return lax.rsqrt(jnp.sum(f * f, axis=1, keepdims=True) + 1e-06)


def triangle_inverse(strict, row, col):
    eye = jnp.where(row == col, 1.0, 0.0)
    diff = row ^ col
    inv = eye - jnp.where(diff == 1, strict, 0.0)
    size = 2
    while size < L:
        below = jnp.where((diff >= size) & (diff < 2 * size), strict, 0.0)
        inv = inv - dot3(inv, dot3(below, inv))
        size *= 2
    return inv


def block_prepare(kr, vr, logit_row):
    row, col = index_grids()
    beta_row = 2.0 * jax.nn.sigmoid(logit_row)
    beta = to_col(beta_row, row, col)
    rk = inv_norm(kr)
    rk_row = to_row(rk, row, col)
    gram = dot1(kr, kr, NT) * rk * rk_row
    strict = jnp.where(row > col, gram * beta_row, 0.0)
    inv = triangle_inverse(strict, row, col)
    solved_k = dot2(inv * rk_row, kr)
    solved_v = dot2(inv, vr)
    scale = beta * rk
    less = dot2(solved_k * scale, kr, TN)
    gain = dot2(solved_v * scale, kr, TN)
    return less, gain, inv, solved_k, solved_v


def block_side(qr, kr, logit_row, inv, solved_k, solved_v):
    row, col = index_grids()
    beta_row = 2.0 * jax.nn.sigmoid(logit_row)
    beta = to_col(beta_row, row, col)
    rk, rq = inv_norm(kr), inv_norm(qr)
    attend = jnp.where(row >= col, dot1(qr, kr, NT) * rq * to_row(rk, row, col), 0.0)
    attend = attend * beta_row
    read = qr.astype(F32) * rq - dot3(attend, solved_k)
    fixed = dot3(attend, solved_v)
    back_out = dot3(attend, inv)
    back_k = dot3(inv, beta * (kr.astype(F32) * rk), TN)
    return read, fixed, back_out, back_k


def block_outputs(ct, start, read, fixed):
    raw = fixed + dot3(read, start, NT)
    rn = lax.rsqrt(jnp.mean(raw * raw, axis=1, keepdims=True) + 1e-05)
    normed = raw * rn
    cotan = ct.astype(F32)
    d_raw = rn * (cotan - normed * jnp.mean(normed * cotan, axis=1, keepdims=True))
    return normed, d_raw, dot3(d_raw, read, TN)


def block_grads_early(qr, kr, logit_row, start, errors, d_raw):
    row, col = index_grids()
    beta = to_col(2.0 * jax.nn.sigmoid(logit_row), row, col)
    rk, rq = inv_norm(kr), inv_norm(qr)
    rk_row = to_row(rk, row, col)
    scaled = beta * errors
    d_attend = jnp.where(row >= col, dot3(d_raw, scaled, NT), 0.0)
    dq_unit = dot3(d_raw, start) + dot2(d_attend * rk_row, kr)
    dk_part = dot2(d_attend * rq, qr, TN)
    q_unit = qr.astype(F32) * rq
    dq = rq * (dq_unit - q_unit * jnp.sum(q_unit * dq_unit, axis=1, keepdims=True))
    return dq, dk_part


def block_logit_grads(logit_row, end_grad, errors, back0, back_k):
    row, col = index_grids()
    keep = to_col(jax.nn.sigmoid(-logit_row), row, col)
    back = back0 + dot3(back_k, end_grad, NT)
    return back, to_row(jnp.sum(errors * back, axis=1, keepdims=True) * keep, row, col)


def block_key_grads(kr, logit_row, start, end_grad, errors, back, dk_part):
    row, col = index_grids()
    beta = to_col(2.0 * jax.nn.sigmoid(logit_row), row, col)
    rk = inv_norm(kr)
    rk_row = to_row(rk, row, col)
    scaled = beta * errors
    d_gram = jnp.where(row > col, -dot3(back, scaled, NT), 0.0)
    d_gram = d_gram + jnp.where(row < col, -dot3(scaled, back, NT), 0.0)
    dk_unit = dk_part - dot3(back, start) + dot3(scaled, end_grad) + dot2(d_gram * rk_row, kr)
    k_unit = kr.astype(F32) * rk
    return rk * (dk_unit - k_unit * jnp.sum(k_unit * dk_unit, axis=1, keepdims=True))


def level_of(x):
    top = jnp.max(jnp.max(jnp.abs(x), axis=1, keepdims=True), axis=0, keepdims=True)
    return jnp.ceil(jnp.log2(jnp.maximum(top, 1e-30)))


def packed(x):
    level = level_of(x)
    return x * jnp.exp2(-level), jnp.broadcast_to(level, (16, D))


def scaled_back(x, level):
    return x * jnp.exp2(level[0:1])


def step(state, less, dims=NN):
    return state - dot3(state, less, dims)


def chain_forward(less, gain, place, count):
    eye = jnp.where(index_grids()[0] == index_grids()[1], 1.0, 0.0)
    zero = jnp.zeros((D, D), F32)
    state = jnp.concatenate([eye, zero], axis=0)
    own = state
    for j in range(count):
        if place is not None:
            own = jnp.where(place == j, state, own)
            if j == count - 1:
                break
        if j == 0:
            state = jnp.concatenate([eye - less(j), gain(j)], axis=0)
        else:
            state = step(state, less(j)) + jnp.concatenate([zero, gain(j)], axis=0)
    return state, own


def chain_state(less, gain, place, count):
    state = jnp.zeros((D, D), F32)
    own = state
    for j in range(count - 1):
        state = gain(j) if j == 0 else step(state, less(j)) + gain(j)
        own = jnp.where(place == j + 1, state, own)
    return own


def chain_back_matrix(less, place, count):
    state = jnp.where(index_grids()[0] == index_grids()[1], 1.0, 0.0)
    own = state
    for j in range(count - 1, 0, -1):
        state = step(state, less(j), NT)
        own = jnp.where(place == j - 1, state, own)
    return own


def chain_back(less, give, place, count, total=True):
    state = jnp.zeros((D, D), F32)
    own = state
    for j in range(count - 1, -1 if total else 0, -1):
        own = jnp.where(place == j, state, own)
        state = give(j) if j == count - 1 else step(state, less(j), NT) + give(j)
    if not total:
        own = jnp.where(place == 0, state, own)
    return state, own


def put(send, less, gain):
    send[0:D] = less
    send[D : 2 * D], send[2 * D : 2 * D + 16] = packed(gain)


def less_of(got):
    return lambda j: got[j, 0:D]


def gain_of(got):
    return lambda j: scaled_back(got[j, D : 2 * D], got[j, 2 * D : 2 * D + 8])


def give_of(got):
    return lambda j: scaled_back(got[j, 0:D], got[j, D : D + 8])


def in_order(side, mine, theirs):
    first = side[0] == 0
    return jnp.where(first, mine, theirs), jnp.where(first, theirs, mine)


def kernel_first(side, slot, bias, weight, hidden, k, v, q, ct, part, mine, theirs,
                 offset, narrow, held, done):
    small = pltpu.make_async_copy(bias, offset, done.at[6])
    small.start()
    copies = [pltpu.make_async_copy(weight, narrow, done.at[5])] + [
        pltpu.make_async_copy(x, held.at[i], done.at[i])
        for i, x in enumerate((hidden, k, v, q, ct))
    ]
    for copy in copies:
        copy.start()
    copies[0].wait()
    copies[1].wait()
    small.wait()
    head = lax.broadcasted_iota(jnp.int32, (16, L), 0) - 2 * slot[0]
    own = jnp.where(head == 0, offset[0], jnp.where(head == 1, offset[1], 0.0))
    part[...] = dot1(narrow[...], held[0], NT) + own
    for i in range(4):
        copies[i + 2].wait()
        mine[i], theirs[i] = in_order(side, held[i + 1, :, :D], held[i + 1, :, D:])
    theirs[4], theirs[5] = held[0, :, :D], held[0, :, D:]


def kernel_prepare(side, part, mine, swapped, send, lg, less, gain, inv, sk, sv):
    odd = lax.broadcasted_iota(jnp.int32, (16, L), 0) % 2
    moves = []
    ks, vs = in_order(side, mine[0], swapped[0]), in_order(side, mine[1], swapped[1])
    for b in range(2):
        logit = jnp.sum(jnp.where(odd == b, part[...], 0.0), axis=0, keepdims=True)
        lg[b : b + 1, :] = logit
        w, n, *rest = block_prepare(ks[b], vs[b], logit)
        less[b], gain[b] = w, n
        inv[b], sk[b], sv[b] = rest
        moves.append((w, n))
    (w0, n0), (w1, n1) = moves
    both = step(jnp.concatenate([w0, n0], axis=0), w1)
    put(send, both[:D] + w1, both[D:] + n1)


def kernel_row_forward(count, got, send):
    state, _ = chain_forward(less_of(got), gain_of(got), None, count)
    row, col = index_grids()
    put(send, jnp.where(row == col, 1.0, 0.0) - state[:D], state[D:])


def kernel_side(count, place, side, lg, mine, swapped, got, inv, sk, sv,
                own, matrix, read, fixed, bo, bk):
    ks, qs = in_order(side, mine[0], swapped[0]), in_order(side, mine[2], swapped[2])
    for b in range(2):
        read[b], fixed[b], bo[b], bk[b] = block_side(
            qs[b], ks[b], lg[b : b + 1, :], inv[b], sk[b], sv[b]
        )
    own[...] = chain_forward(less_of(got), gain_of(got), place[0], count)[1]
    matrix[...] = chain_back_matrix(less_of(got), place[0], count)


def kernel_outputs(count, place, side, got, own, mine, swapped, less, gain, read, fixed,
                   out, start, draw, give, send):
    cs = in_order(side, mine[3], swapped[3])
    first = chain_state(less_of(got), gain_of(got), place[0], count)
    before = dot3(first, own[:D]) + own[D:]
    gives = []
    for b in range(2):
        if b == 1:
            before = step(before, less[0]) + gain[0]
        normed, draw[b], g = block_outputs(cs[b], before, read[b], fixed[b])
        out[b] = normed.astype(BF16)
        start[b] = before
        gives.append(g)
    give[...] = gives[1]
    send[0:D], send[D : D + 16] = packed(step(gives[1], less[0], NT) + gives[0])


def kernel_early(side, lg, own, swapped, start, draw, sk, sv, bo, out,
                 mine, theirs, dkp, err, back0):
    ks, qs = in_order(side, own[0], swapped[0]), in_order(side, own[2], swapped[2])
    dqs = []
    for b in range(2):
        errors = sv[b] - dot3(sk[b], start[b], NT)
        err[b] = errors
        back0[b] = dot3(bo[b], draw[b], TN)
        dq, dkp[b] = block_grads_early(
            qs[b], ks[b], lg[b : b + 1, :], start[b], errors, draw[b]
        )
        dqs.append(dq)
    mine[0], theirs[0] = in_order(side, out[0], out[1])
    dqs = in_order(side, *dqs)
    mine[1], theirs[1] = dqs[0].astype(BF16), dqs[1].astype(BF16)


def kernel_row_back(count, place, got, gives, send, own):
    state, after = chain_back(less_of(got), give_of(gives), place[0], count)
    send[0:D], send[D : D + 16] = packed(state)
    own[...] = after


def kernel_grads(count, place, got, gives, matrix, own, lg, less, give, err, back0, bk,
                 ends, back, message):
    _, row_after = chain_back(less_of(got), give_of(gives), place[0], count, total=False)
    end_grad = dot3(row_after, matrix[...]) + own[...]
    ends[1] = end_grad
    ends[0] = step(end_grad, less[1], NT) + give[...]
    rows = []
    for b in range(2):
        back[b], row = block_logit_grads(lg[b : b + 1, :], ends[b], err[b], back0[b], bk[b])
        rows.append(row)
    odd = lax.broadcasted_iota(jnp.int32, (32, L), 0) % 2
    message[...] = jnp.where(odd == 0, rows[0], rows[1])


def kernel_keys(side, lg, held, swapped, start, ends, err, back, dkp, mine, theirs):
    ks = in_order(side, held[0], swapped[0])
    dks = [
        block_key_grads(ks[b], lg[b : b + 1, :], start[b], ends[b], err[b], back[b], dkp[b])
        for b in range(2)
    ]
    for i, pair in enumerate((dks, (back[0], back[1]))):
        x, y = in_order(side, *pair)
        mine[i], theirs[i] = x.astype(BF16), y.astype(BF16)


def kernel_weight(side, slot, got, hidden, swapped, total, grads):
    rows = [got[pl.ds(b, 16, stride=2), :] for b in range(2)]
    here, there = in_order(side, *rows)
    grads[...] = here.astype(BF16)
    theirs = jnp.concatenate([swapped[4], swapped[5]], axis=1)
    weight = dot1(here.astype(BF16), hidden[...]) + dot1(there.astype(BF16), theirs)
    bias = jnp.sum(rows[0] + rows[1], axis=1, keepdims=True)
    row = lax.broadcasted_iota(jnp.int32, (16, 2 * D), 0)
    col = lax.broadcasted_iota(jnp.int32, (16, 2 * D), 1)
    line = jnp.sum(
        jnp.where((row - 2 * slot[0] == col) & (col < 2), bias, 0.0), axis=0, keepdims=True
    )
    for i in range(total.shape[0]):
        total[i, 0:16] = weight
        total[i, 16:24] = jnp.broadcast_to(line, (8, 2 * D))


VM = pl.BlockSpec(memory_space=pltpu.VMEM)
SM = pl.BlockSpec(memory_space=pltpu.SMEM)


def call(body, outs, *args, flops=1e8):
    specs = [SM if a.ndim == 1 else VM for a in args]
    total = sum(a.size * a.dtype.itemsize for a in args)
    return pl.pallas_call(
        body,
        out_shape=[jax.ShapeDtypeStruct(s, t) for s, t in outs],
        in_specs=specs,
        out_specs=[VM] * len(outs),
        compiler_params=pltpu.CompilerParams(vmem_limit_bytes=16 * 2**20),
        cost_estimate=pl.CostEstimate(flops=int(flops), bytes_accessed=total, transcendentals=0),
    )(*args)


def copies(x, axis):
    count = lax.axis_size(axis)
    return lax.all_to_all(jnp.broadcast_to(x[None], (count,) + x.shape), axis, 0, 0)


def spread(x, axis):
    return copies(x.astype(jnp.float16), axis).astype(F32)


def swap(x):
    return lax.ppermute(x, "zl", [(0, 1), (1, 0)])


def joined(side, mine, theirs):
    return jnp.where(
        side == 0,
        jnp.concatenate([mine, theirs], axis=1),
        jnp.concatenate([theirs, mine], axis=1),
    )


HALF = ((D, D), F32)
PAIR = ((2, D, D), F32)
PAIRB = ((2, L, D), BF16)


def per_device(hidden, beta_weight, beta_bias, queries, keys, values, cotangent):
    rows, pairs = lax.axis_size("y"), lax.axis_size("zh")
    side = lax.axis_index("zl").astype(jnp.int32)
    at_y = lax.axis_index("y").astype(jnp.int32).reshape(1)
    at_z = lax.axis_index("zh").astype(jnp.int32).reshape(1)
    at_s = side.reshape(1)

    at_h = lax.axis_index("head").astype(jnp.int32).reshape(1)

    four, six = [jax.ShapeDtypeStruct((n, L, D), BF16) for n in (4, 6)]
    part, held, theirs = pl.pallas_call(
        kernel_first,
        out_shape=[jax.ShapeDtypeStruct((16, L), F32), four, six],
        in_specs=[SM] * 2 + [pl.BlockSpec(memory_space=pl.ANY)] * 7,
        out_specs=[VM] * 3,
        scratch_shapes=[
            pltpu.SMEM((2,), F32),
            pltpu.VMEM((16, 2 * D), BF16),
            pltpu.VMEM((5, L, 2 * D), BF16),
            pltpu.SemaphoreType.DMA((7,)),
        ],
        compiler_params=pltpu.CompilerParams(vmem_limit_bytes=60 * 2**20),
        cost_estimate=pl.CostEstimate(flops=10**7, bytes_accessed=10**6, transcendentals=0),
    )(at_s, at_h, beta_bias, beta_weight.T, hidden, keys, values, queries, cotangent)
    part = lax.all_to_all(part, ("head", "zl"), 0, 0, tiled=True)
    swapped = swap(theirs)

    send1, logits, less, gain, inv, sk, sv = call(
        kernel_prepare, [((2 * D + 16, D), F32), ((2, L), F32)] + [PAIR] * 5,
        at_s, part, held, swapped,
    )
    got1 = spread(send1, "zh")
    (send2,) = call(
        functools.partial(kernel_row_forward, pairs), [((2 * D + 16, D), F32)], got1
    )
    got2 = spread(send2, "y")
    own1, matrix, read, fixed, bo, bk = call(
        functools.partial(kernel_side, pairs), [((2 * D, D), F32), HALF] + [PAIR] * 4,
        at_z, at_s, logits, held, swapped, got1, inv, sk, sv,
    )
    out, start, draw, give, send3 = call(
        functools.partial(kernel_outputs, rows),
        [PAIRB] + [PAIR] * 2 + [HALF, ((D + 16, D), F32)],
        at_y, at_s, got2, own1, held, swapped, less, gain, read, fixed,
    )
    got3 = spread(send3, "zh")
    mine, theirs, dkp, err, back0 = call(
        kernel_early, [PAIRB, PAIRB] + [PAIR] * 3,
        at_s, logits, held, swapped, start, draw, sk, sv, bo, out,
    )
    send4, own2 = call(
        functools.partial(kernel_row_back, pairs), [((D + 16, D), F32), HALF], at_z, got1, got3
    )
    got4 = spread(send4, "y")
    theirs = swap(theirs)
    ends, back, message = call(
        functools.partial(kernel_grads, rows), [PAIR, PAIR, ((32, L), F32)],
        at_y, got2, got4, matrix, own2, logits, less, give, err, back0, bk,
    )
    mine_kv, theirs_kv = call(
        kernel_keys, [PAIRB, PAIRB],
        at_s, logits, held, swapped, start, ends, err, back, dkp,
    )

    message = lax.all_to_all(message.reshape(16, 2, L), ("head", "zl"), 0, 0)
    total, grads = call(
        kernel_weight, [((pairs, 24, 2 * D), F32), ((16, L), BF16)],
        at_s, at_h, message.reshape(32, L), hidden, swapped,
    )
    total, theirs_kv = lax.optimization_barrier((total, theirs_kv))
    total = jnp.sum(lax.all_to_all(total, "zh", 0, 0), axis=0)
    total = jnp.sum(copies(total, "y"), axis=0)
    theirs_kv = swap(theirs_kv)
    d_hidden = lax.dot_general(
        grads, beta_weight, (((0,), (1,)), ((), ())), preferred_element_type=F32
    )
    out, dq = [joined(side, mine[i], theirs[i]) for i in range(2)]
    dk, dv = [joined(side, mine_kv[i], theirs_kv[i]) for i in range(2)]
    return (out, dq, dk, dv, d_hidden.astype(BF16), total[:16].T, total[16, 0:2])


def solution(mesh):
    grid = Mesh(mesh.devices.reshape(8, 6, 2, 8), ("y", "zh", "zl", "head"))
    seq = P(("y", "zh", "zl"), "head")
    return jax.shard_map(
        per_device,
        mesh=grid,
        in_specs=(seq, P("head", None), P("head"), seq, seq, seq, seq),
        out_specs=(seq, seq, seq, seq, seq, P("head", None), P("head")),
        check_vma=False,
    )
```

```python
import functools

import jax
import jax.numpy as jnp
from jax import lax
from jax.experimental import pallas as pl
from jax.experimental.pallas import tpu as pltpu
from jax.sharding import Mesh, PartitionSpec as P

F32 = jnp.float32
BF16 = jnp.bfloat16
L = 128
D = 128
NN = (((1,), (0,)), ((), ()))
NT = (((1,), (1,)), ((), ()))
TN = (((0,), (0,)), ((), ()))


def dot1(a, b, dims=NN):
    return lax.dot_general(a, b, dims, preferred_element_type=F32)


def split(x):
    hi = x.astype(BF16)
    return hi, (x - hi.astype(F32)).astype(BF16)


def along(dims, a_parts, b_parts):
    return dot1(
        jnp.concatenate(a_parts, axis=dims[0][0][0]),
        jnp.concatenate(b_parts, axis=dims[0][1][0]),
        dims,
    )


def dot2(a, b, dims=NN):
    hi, lo = split(a)
    return along(dims, [hi, lo], [b, b])


def dot3(a, b, dims=NN):
    ah, al = split(a)
    bh, bl = split(b)
    return along(dims, [ah, al, ah], [bh, bh, bl])


def index_grids():
    row = lax.broadcasted_iota(jnp.int32, (L, L), 0)
    col = lax.broadcasted_iota(jnp.int32, (L, L), 1)
    return row, col


def to_col(row_vec, row, col):
    return jnp.sum(jnp.where(row == col, row_vec, 0.0), axis=1, keepdims=True)


def to_row(col_vec, row, col):
    return jnp.sum(jnp.where(row == col, col_vec, 0.0), axis=0, keepdims=True)


def inv_norm(raw):
    f = raw.astype(F32)
    return lax.rsqrt(jnp.sum(f * f, axis=1, keepdims=True) + 1e-06)


def triangle_inverse(strict, row, col):
    eye = jnp.where(row == col, 1.0, 0.0)
    diff = row ^ col
    inv = eye - jnp.where(diff == 1, strict, 0.0)
    size = 2
    while size < L:
        below = jnp.where((diff >= size) & (diff < 2 * size), strict, 0.0)
        inv = inv - dot3(inv, dot3(below, inv))
        size *= 2
    return inv


def block_prepare(kr, vr, logit_row):
    row, col = index_grids()
    beta_row = 2.0 * jax.nn.sigmoid(logit_row)
    beta = to_col(beta_row, row, col)
    rk = inv_norm(kr)
    rk_row = to_row(rk, row, col)
    gram = dot1(kr, kr, NT) * rk * rk_row
    strict = jnp.where(row > col, gram * beta_row, 0.0)
    inv = triangle_inverse(strict, row, col)
    solved_k = dot2(inv * rk_row, kr)
    solved_v = dot2(inv, vr)
    scale = beta * rk
    less = dot2(solved_k * scale, kr, TN)
    gain = dot2(solved_v * scale, kr, TN)
    return less, gain, inv, solved_k, solved_v


def block_side(qr, kr, logit_row, inv, solved_k, solved_v):
    row, col = index_grids()
    beta_row = 2.0 * jax.nn.sigmoid(logit_row)
    beta = to_col(beta_row, row, col)
    rk, rq = inv_norm(kr), inv_norm(qr)
    attend = jnp.where(row >= col, dot1(qr, kr, NT) * rq * to_row(rk, row, col), 0.0)
    attend = attend * beta_row
    read = qr.astype(F32) * rq - dot3(attend, solved_k)
    fixed = dot3(attend, solved_v)
    back_out = dot3(attend, inv)
    back_k = dot3(inv, beta * (kr.astype(F32) * rk), TN)
    return read, fixed, back_out, back_k


def block_outputs(ct, start, read, fixed):
    raw = fixed + dot3(read, start, NT)
    rn = lax.rsqrt(jnp.mean(raw * raw, axis=1, keepdims=True) + 1e-05)
    normed = raw * rn
    cotan = ct.astype(F32)
    d_raw = rn * (cotan - normed * jnp.mean(normed * cotan, axis=1, keepdims=True))
    return normed, d_raw, dot3(d_raw, read, TN)


def block_grads_early(qr, kr, logit_row, start, errors, d_raw):
    row, col = index_grids()
    beta = to_col(2.0 * jax.nn.sigmoid(logit_row), row, col)
    rk, rq = inv_norm(kr), inv_norm(qr)
    rk_row = to_row(rk, row, col)
    scaled = beta * errors
    d_attend = jnp.where(row >= col, dot3(d_raw, scaled, NT), 0.0)
    dq_unit = dot3(d_raw, start) + dot2(d_attend * rk_row, kr)
    dk_part = dot2(d_attend * rq, qr, TN)
    q_unit = qr.astype(F32) * rq
    dq = rq * (dq_unit - q_unit * jnp.sum(q_unit * dq_unit, axis=1, keepdims=True))
    return dq, dk_part


def block_logit_grads(logit_row, end_grad, errors, back0, back_k):
    row, col = index_grids()
    keep = to_col(jax.nn.sigmoid(-logit_row), row, col)
    back = back0 + dot3(back_k, end_grad, NT)
    return back, to_row(jnp.sum(errors * back, axis=1, keepdims=True) * keep, row, col)


def block_key_grads(kr, logit_row, start, end_grad, errors, back, dk_part):
    row, col = index_grids()
    beta = to_col(2.0 * jax.nn.sigmoid(logit_row), row, col)
    rk = inv_norm(kr)
    rk_row = to_row(rk, row, col)
    scaled = beta * errors
    d_gram = jnp.where(row > col, -dot3(back, scaled, NT), 0.0)
    d_gram = d_gram + jnp.where(row < col, -dot3(scaled, back, NT), 0.0)
    dk_unit = dk_part - dot3(back, start) + dot3(scaled, end_grad) + dot2(d_gram * rk_row, kr)
    k_unit = kr.astype(F32) * rk
    return rk * (dk_unit - k_unit * jnp.sum(k_unit * dk_unit, axis=1, keepdims=True))


def level_of(x):
    top = jnp.max(jnp.max(jnp.abs(x), axis=1, keepdims=True), axis=0, keepdims=True)
    return jnp.ceil(jnp.log2(jnp.maximum(top, 1e-30)))


def packed(x):
    level = level_of(x)
    return x * jnp.exp2(-level), jnp.broadcast_to(level, (16, D))


def scaled_back(x, level):
    return x * jnp.exp2(level[0:1])


def step(state, less, dims=NN):
    return state - dot3(state, less, dims)


def chain_forward(less, gain, place, count):
    eye = jnp.where(index_grids()[0] == index_grids()[1], 1.0, 0.0)
    zero = jnp.zeros((D, D), F32)
    state = jnp.concatenate([eye, zero], axis=0)
    own = state
    for j in range(count):
        if place is not None:
            own = jnp.where(place == j, state, own)
            if j == count - 1:
                break
        if j == 0:
            state = jnp.concatenate([eye - less(j), gain(j)], axis=0)
        else:
            state = step(state, less(j)) + jnp.concatenate([zero, gain(j)], axis=0)
    return state, own


def chain_state(less, gain, place, count):
    state = jnp.zeros((D, D), F32)
    own = state
    for j in range(count - 1):
        state = gain(j) if j == 0 else step(state, less(j)) + gain(j)
        own = jnp.where(place == j + 1, state, own)
    return own


def chain_back_matrix(less, place, count):
    state = jnp.where(index_grids()[0] == index_grids()[1], 1.0, 0.0)
    own = state
    for j in range(count - 1, 0, -1):
        state = step(state, less(j), NT)
        own = jnp.where(place == j - 1, state, own)
    return own


def chain_back(less, give, place, count, total=True):
    state = jnp.zeros((D, D), F32)
    own = state
    for j in range(count - 1, -1 if total else 0, -1):
        own = jnp.where(place == j, state, own)
        state = give(j) if j == count - 1 else step(state, less(j), NT) + give(j)
    if not total:
        own = jnp.where(place == 0, state, own)
    return state, own


def put(send, less, gain):
    send[0:D] = less
    send[D : 2 * D], send[2 * D : 2 * D + 16] = packed(gain)


def less_of(got):
    return lambda j: got[j, 0:D]


def gain_of(got):
    return lambda j: scaled_back(got[j, D : 2 * D], got[j, 2 * D : 2 * D + 8])


def give_of(got):
    return lambda j: scaled_back(got[j, 0:D], got[j, D : D + 8])


def in_order(side, mine, theirs):
    first = side[0] == 0
    return jnp.where(first, mine, theirs), jnp.where(first, theirs, mine)


def kernel_first(side, slot, bias, weight, hidden, k, v, q, ct, part, mine, theirs,
                 offset, narrow, held, done):
    small = pltpu.make_async_copy(bias, offset, done.at[6])
    small.start()
    copies = [pltpu.make_async_copy(weight, narrow, done.at[5])] + [
        pltpu.make_async_copy(x, held.at[i], done.at[i])
        for i, x in enumerate((hidden, k, v, q, ct))
    ]
    for copy in copies:
        copy.start()
    copies[0].wait()
    copies[1].wait()
    small.wait()
    head = lax.broadcasted_iota(jnp.int32, (16, L), 0) - 2 * slot[0]
    own = jnp.where(head == 0, offset[0], jnp.where(head == 1, offset[1], 0.0))
    part[...] = dot1(narrow[...], held[0], NT) + own
    for i in range(4):
        copies[i + 2].wait()
        mine[i], theirs[i] = in_order(side, held[i + 1, :, :D], held[i + 1, :, D:])
    theirs[4], theirs[5] = held[0, :, :D], held[0, :, D:]


def kernel_prepare(side, part, mine, swapped, send, lg, less, gain, inv, sk, sv):
    odd = lax.broadcasted_iota(jnp.int32, (16, L), 0) % 2
    moves = []
    ks, vs = in_order(side, mine[0], swapped[0]), in_order(side, mine[1], swapped[1])
    for b in range(2):
        logit = jnp.sum(jnp.where(odd == b, part[...], 0.0), axis=0, keepdims=True)
        lg[b : b + 1, :] = logit
        w, n, *rest = block_prepare(ks[b], vs[b], logit)
        less[b], gain[b] = w, n
        inv[b], sk[b], sv[b] = rest
        moves.append((w, n))
    (w0, n0), (w1, n1) = moves
    both = step(jnp.concatenate([w0, n0], axis=0), w1)
    put(send, both[:D] + w1, both[D:] + n1)


def kernel_row_forward(count, got, send):
    state, _ = chain_forward(less_of(got), gain_of(got), None, count)
    row, col = index_grids()
    put(send, jnp.where(row == col, 1.0, 0.0) - state[:D], state[D:])


def kernel_side(count, place, side, lg, mine, swapped, got, inv, sk, sv,
                own, matrix, read, fixed, bo, bk):
    ks, qs = in_order(side, mine[0], swapped[0]), in_order(side, mine[2], swapped[2])
    for b in range(2):
        read[b], fixed[b], bo[b], bk[b] = block_side(
            qs[b], ks[b], lg[b : b + 1, :], inv[b], sk[b], sv[b]
        )
    own[...] = chain_forward(less_of(got), gain_of(got), place[0], count)[1]
    matrix[...] = chain_back_matrix(less_of(got), place[0], count)


def kernel_outputs(count, place, side, got, own, mine, swapped, less, gain, read, fixed,
                   out, start, draw, give, send):
    cs = in_order(side, mine[3], swapped[3])
    first = chain_state(less_of(got), gain_of(got), place[0], count)
    before = dot3(first, own[:D]) + own[D:]
    gives = []
    for b in range(2):
        if b == 1:
            before = step(before, less[0]) + gain[0]
        normed, draw[b], g = block_outputs(cs[b], before, read[b], fixed[b])
        out[b] = normed.astype(BF16)
        start[b] = before
        gives.append(g)
    give[...] = gives[1]
    send[0:D], send[D : D + 16] = packed(step(gives[1], less[0], NT) + gives[0])


def kernel_early(side, lg, own, swapped, start, draw, sk, sv, bo, out,
                 mine, theirs, dkp, err, back0):
    ks, qs = in_order(side, own[0], swapped[0]), in_order(side, own[2], swapped[2])
    dqs = []
    for b in range(2):
        errors = sv[b] - dot3(sk[b], start[b], NT)
        err[b] = errors
        back0[b] = dot3(bo[b], draw[b], TN)
        dq, dkp[b] = block_grads_early(
            qs[b], ks[b], lg[b : b + 1, :], start[b], errors, draw[b]
        )
        dqs.append(dq)
    mine[0], theirs[0] = in_order(side, out[0], out[1])
    dqs = in_order(side, *dqs)
    mine[1], theirs[1] = dqs[0].astype(BF16), dqs[1].astype(BF16)


def kernel_row_back(count, place, got, gives, send, own):
    state, after = chain_back(less_of(got), give_of(gives), place[0], count)
    send[0:D], send[D : D + 16] = packed(state)
    own[...] = after


def kernel_grads(count, place, got, gives, matrix, own, lg, less, give, err, back0, bk,
                 ends, back, message):
    _, row_after = chain_back(less_of(got), give_of(gives), place[0], count, total=False)
    end_grad = dot3(row_after, matrix[...]) + own[...]
    ends[1] = end_grad
    ends[0] = step(end_grad, less[1], NT) + give[...]
    rows = []
    for b in range(2):
        back[b], row = block_logit_grads(lg[b : b + 1, :], ends[b], err[b], back0[b], bk[b])
        rows.append(row)
    odd = lax.broadcasted_iota(jnp.int32, (32, L), 0) % 2
    message[...] = jnp.where(odd == 0, rows[0], rows[1])


def kernel_keys(side, lg, held, swapped, start, ends, err, back, dkp, mine, theirs):
    ks = in_order(side, held[0], swapped[0])
    dks = [
        block_key_grads(ks[b], lg[b : b + 1, :], start[b], ends[b], err[b], back[b], dkp[b])
        for b in range(2)
    ]
    for i, pair in enumerate((dks, (back[0], back[1]))):
        x, y = in_order(side, *pair)
        mine[i], theirs[i] = x.astype(BF16), y.astype(BF16)


def kernel_weight(side, slot, got, hidden, swapped, total, grads):
    rows = [got[pl.ds(b, 16, stride=2), :] for b in range(2)]
    here, there = in_order(side, *rows)
    grads[...] = here.astype(BF16)
    theirs = jnp.concatenate([swapped[4], swapped[5]], axis=1)
    weight = dot1(here.astype(BF16), hidden[...]) + dot1(there.astype(BF16), theirs)
    bias = jnp.sum(rows[0] + rows[1], axis=1, keepdims=True)
    row = lax.broadcasted_iota(jnp.int32, (16, 2 * D), 0)
    col = lax.broadcasted_iota(jnp.int32, (16, 2 * D), 1)
    line = jnp.sum(
        jnp.where((row - 2 * slot[0] == col) & (col < 2), bias, 0.0), axis=0, keepdims=True
    )
    for i in range(total.shape[0]):
        total[i, 0:16] = weight
        total[i, 16:24] = jnp.broadcast_to(line, (8, 2 * D))


VM = pl.BlockSpec(memory_space=pltpu.VMEM)
SM = pl.BlockSpec(memory_space=pltpu.SMEM)


def call(body, outs, *args, flops=1e8):
    specs = [SM if a.ndim == 1 else VM for a in args]
    total = sum(a.size * a.dtype.itemsize for a in args)
    return pl.pallas_call(
        body,
        out_shape=[jax.ShapeDtypeStruct(s, t) for s, t in outs],
        in_specs=specs,
        out_specs=[VM] * len(outs),
        compiler_params=pltpu.CompilerParams(vmem_limit_bytes=16 * 2**20),
        cost_estimate=pl.CostEstimate(flops=int(flops), bytes_accessed=total, transcendentals=0),
    )(*args)


def copies(x, axis):
    count = lax.axis_size(axis)
    return lax.all_to_all(jnp.broadcast_to(x[None], (count,) + x.shape), axis, 0, 0)


def spread(x, axis):
    return copies(x.astype(jnp.float16), axis).astype(F32)


def swap(x):
    return lax.ppermute(x, "zl", [(0, 1), (1, 0)])


def joined(side, mine, theirs):
    return jnp.where(
        side == 0,
        jnp.concatenate([mine, theirs], axis=1),
        jnp.concatenate([theirs, mine], axis=1),
    )


HALF = ((D, D), F32)
PAIR = ((2, D, D), F32)
PAIRB = ((2, L, D), BF16)


def per_device(hidden, beta_weight, beta_bias, queries, keys, values, cotangent):
    rows, pairs = lax.axis_size("y"), lax.axis_size("zh")
    side = lax.axis_index("zl").astype(jnp.int32)
    at_y = lax.axis_index("y").astype(jnp.int32).reshape(1)
    at_z = lax.axis_index("zh").astype(jnp.int32).reshape(1)
    at_s = side.reshape(1)

    at_h = lax.axis_index("head").astype(jnp.int32).reshape(1)

    four, six = [jax.ShapeDtypeStruct((n, L, D), BF16) for n in (4, 6)]
    part, held, theirs = pl.pallas_call(
        kernel_first,
        out_shape=[jax.ShapeDtypeStruct((16, L), F32), four, six],
        in_specs=[SM] * 2 + [pl.BlockSpec(memory_space=pl.ANY)] * 7,
        out_specs=[VM] * 3,
        scratch_shapes=[
            pltpu.SMEM((2,), F32),
            pltpu.VMEM((16, 2 * D), BF16),
            pltpu.VMEM((5, L, 2 * D), BF16),
            pltpu.SemaphoreType.DMA((7,)),
        ],
        compiler_params=pltpu.CompilerParams(vmem_limit_bytes=60 * 2**20),
        cost_estimate=pl.CostEstimate(flops=10**7, bytes_accessed=10**6, transcendentals=0),
    )(at_s, at_h, beta_bias, beta_weight.T, hidden, keys, values, queries, cotangent)
    part = lax.all_to_all(part, ("head", "zl"), 0, 0, tiled=True)
    swapped = swap(theirs)

    send1, logits, less, gain, inv, sk, sv = call(
        kernel_prepare, [((2 * D + 16, D), F32), ((2, L), F32)] + [PAIR] * 5,
        at_s, part, held, swapped,
    )
    got1 = spread(send1, "zh")
    (send2,) = call(
        functools.partial(kernel_row_forward, pairs), [((2 * D + 16, D), F32)], got1
    )
    got2 = spread(send2, "y")
    own1, matrix, read, fixed, bo, bk = call(
        functools.partial(kernel_side, pairs), [((2 * D, D), F32), HALF] + [PAIR] * 4,
        at_z, at_s, logits, held, swapped, got1, inv, sk, sv,
    )
    out, start, draw, give, send3 = call(
        functools.partial(kernel_outputs, rows),
        [PAIRB] + [PAIR] * 2 + [HALF, ((D + 16, D), F32)],
        at_y, at_s, got2, own1, held, swapped, less, gain, read, fixed,
    )
    got3 = spread(send3, "zh")
    mine, theirs, dkp, err, back0 = call(
        kernel_early, [PAIRB, PAIRB] + [PAIR] * 3,
        at_s, logits, held, swapped, start, draw, sk, sv, bo, out,
    )
    send4, own2 = call(
        functools.partial(kernel_row_back, pairs), [((D + 16, D), F32), HALF], at_z, got1, got3
    )
    got4 = spread(send4, "y")
    theirs = swap(theirs)
    ends, back, message = call(
        functools.partial(kernel_grads, rows), [PAIR, PAIR, ((32, L), F32)],
        at_y, got2, got4, matrix, own2, logits, less, give, err, back0, bk,
    )
    mine_kv, theirs_kv = call(
        kernel_keys, [PAIRB, PAIRB],
        at_s, logits, held, swapped, start, ends, err, back, dkp,
    )

    message = lax.all_to_all(message.reshape(16, 2, L), ("head", "zl"), 0, 0)
    total, grads = call(
        kernel_weight, [((pairs, 24, 2 * D), F32), ((16, L), BF16)],
        at_s, at_h, message.reshape(32, L), hidden, swapped,
    )
    total, theirs_kv = lax.optimization_barrier((total, theirs_kv))
    total = jnp.sum(lax.all_to_all(total, "zh", 0, 0), axis=0)
    total = jnp.sum(copies(total, "y"), axis=0)
    theirs_kv = swap(theirs_kv)
    d_hidden = lax.dot_general(
        grads, beta_weight, (((0,), (1,)), ((), ())), preferred_element_type=F32
    )
    out, dq = [joined(side, mine[i], theirs[i]) for i in range(2)]
    dk, dv = [joined(side, mine_kv[i], theirs_kv[i]) for i in range(2)]
    return (out, dq, dk, dv, d_hidden.astype(BF16), total[:16].T, total[16, 0:2])


def solution(mesh):
    grid = Mesh(mesh.devices.reshape(8, 6, 2, 8), ("y", "zh", "zl", "head"))
    seq = P(("y", "zh", "zl"), "head")
    return jax.shard_map(
        per_device,
        mesh=grid,
        in_specs=(seq, P("head", None), P("head"), seq, seq, seq, seq),
        out_specs=(seq, seq, seq, seq, seq, P("head", None), P("head")),
        check_vma=False,
    )
```

```python
import functools

import jax
import jax.numpy as jnp
from jax import lax
from jax.experimental import pallas as pl
from jax.experimental.pallas import tpu as pltpu
from jax.sharding import Mesh, PartitionSpec as P

F32 = jnp.float32
BF16 = jnp.bfloat16
L = 128
D = 128
NN = (((1,), (0,)), ((), ()))
NT = (((1,), (1,)), ((), ()))
TN = (((0,), (0,)), ((), ()))


def dot1(a, b, dims=NN):
    return lax.dot_general(a, b, dims, preferred_element_type=F32)


def split(x):
    hi = x.astype(BF16)
    return hi, (x - hi.astype(F32)).astype(BF16)


def along(dims, a_parts, b_parts):
    return dot1(
        jnp.concatenate(a_parts, axis=dims[0][0][0]),
        jnp.concatenate(b_parts, axis=dims[0][1][0]),
        dims,
    )


def dot2(a, b, dims=NN):
    hi, lo = split(a)
    return along(dims, [hi, lo], [b, b])


def dot3(a, b, dims=NN):
    ah, al = split(a)
    bh, bl = split(b)
    return along(dims, [ah, al, ah], [bh, bh, bl])


def index_grids():
    row = lax.broadcasted_iota(jnp.int32, (L, L), 0)
    col = lax.broadcasted_iota(jnp.int32, (L, L), 1)
    return row, col


def to_col(row_vec, row, col):
    return jnp.sum(jnp.where(row == col, row_vec, 0.0), axis=1, keepdims=True)


def to_row(col_vec, row, col):
    return jnp.sum(jnp.where(row == col, col_vec, 0.0), axis=0, keepdims=True)


def inv_norm(raw):
    f = raw.astype(F32)
    return lax.rsqrt(jnp.sum(f * f, axis=1, keepdims=True) + 1e-06)


def triangle_inverse(strict, row, col):
    eye = jnp.where(row == col, 1.0, 0.0)
    diff = row ^ col
    inv = eye - jnp.where(diff == 1, strict, 0.0)
    size = 2
    while size < L:
        below = jnp.where((diff >= size) & (diff < 2 * size), strict, 0.0)
        inv = inv - dot3(inv, dot3(below, inv))
        size *= 2
    return inv


def block_prepare(kr, vr, logit_row):
    row, col = index_grids()
    beta_row = 2.0 * jax.nn.sigmoid(logit_row)
    beta = to_col(beta_row, row, col)
    rk = inv_norm(kr)
    rk_row = to_row(rk, row, col)
    gram = dot1(kr, kr, NT) * rk * rk_row
    strict = jnp.where(row > col, gram * beta_row, 0.0)
    inv = triangle_inverse(strict, row, col)
    solved_k = dot2(inv * rk_row, kr)
    solved_v = dot2(inv, vr)
    scale = beta * rk
    less = dot2(solved_k * scale, kr, TN)
    gain = dot2(solved_v * scale, kr, TN)
    return less, gain, inv, solved_k, solved_v


def block_side(qr, kr, logit_row, inv, solved_k, solved_v):
    row, col = index_grids()
    beta_row = 2.0 * jax.nn.sigmoid(logit_row)
    beta = to_col(beta_row, row, col)
    rk, rq = inv_norm(kr), inv_norm(qr)
    attend = jnp.where(row >= col, dot1(qr, kr, NT) * rq * to_row(rk, row, col), 0.0)
    attend = attend * beta_row
    read = qr.astype(F32) * rq - dot3(attend, solved_k)
    fixed = dot3(attend, solved_v)
    back_out = dot3(attend, inv)
    back_k = dot3(inv, beta * (kr.astype(F32) * rk), TN)
    return read, fixed, back_out, back_k


def block_outputs(ct, start, read, fixed):
    raw = fixed + dot3(read, start, NT)
    rn = lax.rsqrt(jnp.mean(raw * raw, axis=1, keepdims=True) + 1e-05)
    normed = raw * rn
    cotan = ct.astype(F32)
    d_raw = rn * (cotan - normed * jnp.mean(normed * cotan, axis=1, keepdims=True))
    return normed, d_raw, dot3(d_raw, read, TN)


def block_grads_early(qr, kr, logit_row, start, errors, d_raw):
    row, col = index_grids()
    beta = to_col(2.0 * jax.nn.sigmoid(logit_row), row, col)
    rk, rq = inv_norm(kr), inv_norm(qr)
    rk_row = to_row(rk, row, col)
    scaled = beta * errors
    d_attend = jnp.where(row >= col, dot3(d_raw, scaled, NT), 0.0)
    dq_unit = dot3(d_raw, start) + dot2(d_attend * rk_row, kr)
    dk_part = dot2(d_attend * rq, qr, TN)
    q_unit = qr.astype(F32) * rq
    dq = rq * (dq_unit - q_unit * jnp.sum(q_unit * dq_unit, axis=1, keepdims=True))
    return dq, dk_part


def block_logit_grads(logit_row, end_grad, errors, back0, back_k):
    row, col = index_grids()
    keep = to_col(jax.nn.sigmoid(-logit_row), row, col)
    back = back0 + dot3(back_k, end_grad, NT)
    return back, to_row(jnp.sum(errors * back, axis=1, keepdims=True) * keep, row, col)


def block_key_grads(kr, logit_row, start, end_grad, errors, back, dk_part):
    row, col = index_grids()
    beta = to_col(2.0 * jax.nn.sigmoid(logit_row), row, col)
    rk = inv_norm(kr)
    rk_row = to_row(rk, row, col)
    scaled = beta * errors
    d_gram = jnp.where(row > col, -dot3(back, scaled, NT), 0.0)
    d_gram = d_gram + jnp.where(row < col, -dot3(scaled, back, NT), 0.0)
    dk_unit = dk_part - dot3(back, start) + dot3(scaled, end_grad) + dot2(d_gram * rk_row, kr)
    k_unit = kr.astype(F32) * rk
    return rk * (dk_unit - k_unit * jnp.sum(k_unit * dk_unit, axis=1, keepdims=True))


def level_of(x):
    top = jnp.max(jnp.max(jnp.abs(x), axis=1, keepdims=True), axis=0, keepdims=True)
    return jnp.ceil(jnp.log2(jnp.maximum(top, 1e-30)))


def packed(x):
    level = level_of(x)
    return x * jnp.exp2(-level), jnp.broadcast_to(level, (16, D))


def scaled_back(x, level):
    return x * jnp.exp2(level[0:1])


def step(state, less, dims=NN):
    return state - dot3(state, less, dims)


def chain_forward(less, gain, place, count):
    eye = jnp.where(index_grids()[0] == index_grids()[1], 1.0, 0.0)
    zero = jnp.zeros((D, D), F32)
    state = jnp.concatenate([eye, zero], axis=0)
    own = state
    for j in range(count):
        if place is not None:
            own = jnp.where(place == j, state, own)
            if j == count - 1:
                break
        if j == 0:
            state = jnp.concatenate([eye - less(j), gain(j)], axis=0)
        else:
            state = step(state, less(j)) + jnp.concatenate([zero, gain(j)], axis=0)
    return state, own


def chain_state(less, gain, place, count):
    state = jnp.zeros((D, D), F32)
    own = state
    for j in range(count - 1):
        state = gain(j) if j == 0 else step(state, less(j)) + gain(j)
        own = jnp.where(place == j + 1, state, own)
    return own


def chain_back_matrix(less, place, count):
    state = jnp.where(index_grids()[0] == index_grids()[1], 1.0, 0.0)
    own = state
    for j in range(count - 1, 0, -1):
        state = step(state, less(j), NT)
        own = jnp.where(place == j - 1, state, own)
    return own


def chain_back(less, give, place, count, total=True):
    state = jnp.zeros((D, D), F32)
    own = state
    for j in range(count - 1, -1 if total else 0, -1):
        own = jnp.where(place == j, state, own)
        state = give(j) if j == count - 1 else step(state, less(j), NT) + give(j)
    if not total:
        own = jnp.where(place == 0, state, own)
    return state, own


def put(send, less, gain):
    send[0:D] = less
    send[D : 2 * D], send[2 * D : 2 * D + 16] = packed(gain)


def less_of(got):
    return lambda j: got[j, 0:D]


def gain_of(got):
    return lambda j: scaled_back(got[j, D : 2 * D], got[j, 2 * D : 2 * D + 8])


def give_of(got):
    return lambda j: scaled_back(got[j, 0:D], got[j, D : D + 8])


def in_order(side, mine, theirs):
    first = side[0] == 0
    return jnp.where(first, mine, theirs), jnp.where(first, theirs, mine)


def kernel_first(side, slot, bias, weight, hidden, k, v, q, ct, part, mine, theirs,
                 offset, narrow, held, done):
    small = pltpu.make_async_copy(bias, offset, done.at[6])
    small.start()
    copies = [pltpu.make_async_copy(weight, narrow, done.at[5])] + [
        pltpu.make_async_copy(x, held.at[i], done.at[i])
        for i, x in enumerate((hidden, k, v, q, ct))
    ]
    for copy in copies:
        copy.start()
    copies[0].wait()
    copies[1].wait()
    small.wait()
    head = lax.broadcasted_iota(jnp.int32, (16, L), 0) - 2 * slot[0]
    own = jnp.where(head == 0, offset[0], jnp.where(head == 1, offset[1], 0.0))
    part[...] = dot1(narrow[...], held[0], NT) + own
    for i in range(4):
        copies[i + 2].wait()
        mine[i], theirs[i] = in_order(side, held[i + 1, :, :D], held[i + 1, :, D:])
    theirs[4], theirs[5] = held[0, :, :D], held[0, :, D:]


def kernel_prepare(side, part, mine, swapped, send, lg, less, gain, inv, sk, sv):
    odd = lax.broadcasted_iota(jnp.int32, (16, L), 0) % 2
    moves = []
    ks, vs = in_order(side, mine[0], swapped[0]), in_order(side, mine[1], swapped[1])
    for b in range(2):
        logit = jnp.sum(jnp.where(odd == b, part[...], 0.0), axis=0, keepdims=True)
        lg[b : b + 1, :] = logit
        w, n, *rest = block_prepare(ks[b], vs[b], logit)
        less[b], gain[b] = w, n
        inv[b], sk[b], sv[b] = rest
        moves.append((w, n))
    (w0, n0), (w1, n1) = moves
    both = step(jnp.concatenate([w0, n0], axis=0), w1)
    put(send, both[:D] + w1, both[D:] + n1)


def kernel_row_forward(count, got, send):
    state, _ = chain_forward(less_of(got), gain_of(got), None, count)
    row, col = index_grids()
    put(send, jnp.where(row == col, 1.0, 0.0) - state[:D], state[D:])


def kernel_side(count, place, side, lg, mine, swapped, got, inv, sk, sv,
                own, matrix, read, fixed, bo, bk):
    ks, qs = in_order(side, mine[0], swapped[0]), in_order(side, mine[2], swapped[2])
    for b in range(2):
        read[b], fixed[b], bo[b], bk[b] = block_side(
            qs[b], ks[b], lg[b : b + 1, :], inv[b], sk[b], sv[b]
        )
    own[...] = chain_forward(less_of(got), gain_of(got), place[0], count)[1]
    matrix[...] = chain_back_matrix(less_of(got), place[0], count)


def kernel_outputs(count, place, side, got, own, mine, swapped, less, gain, read, fixed,
                   out, start, draw, give, send):
    cs = in_order(side, mine[3], swapped[3])
    first = chain_state(less_of(got), gain_of(got), place[0], count)
    before = dot3(first, own[:D]) + own[D:]
    gives = []
    for b in range(2):
        if b == 1:
            before = step(before, less[0]) + gain[0]
        normed, draw[b], g = block_outputs(cs[b], before, read[b], fixed[b])
        out[b] = normed.astype(BF16)
        start[b] = before
        gives.append(g)
    give[...] = gives[1]
    send[0:D], send[D : D + 16] = packed(step(gives[1], less[0], NT) + gives[0])


def kernel_early(side, lg, own, swapped, start, draw, sk, sv, bo, out,
                 mine, theirs, dkp, err, back0):
    ks, qs = in_order(side, own[0], swapped[0]), in_order(side, own[2], swapped[2])
    dqs = []
    for b in range(2):
        errors = sv[b] - dot3(sk[b], start[b], NT)
        err[b] = errors
        back0[b] = dot3(bo[b], draw[b], TN)
        dq, dkp[b] = block_grads_early(
            qs[b], ks[b], lg[b : b + 1, :], start[b], errors, draw[b]
        )
        dqs.append(dq)
    mine[0], theirs[0] = in_order(side, out[0], out[1])
    dqs = in_order(side, *dqs)
    mine[1], theirs[1] = dqs[0].astype(BF16), dqs[1].astype(BF16)


def kernel_row_back(count, place, got, gives, send, own):
    state, after = chain_back(less_of(got), give_of(gives), place[0], count)
    send[0:D], send[D : D + 16] = packed(state)
    own[...] = after


def kernel_grads(count, place, got, gives, matrix, own, lg, less, give, err, back0, bk,
                 ends, back, message):
    _, row_after = chain_back(less_of(got), give_of(gives), place[0], count, total=False)
    end_grad = dot3(row_after, matrix[...]) + own[...]
    ends[1] = end_grad
    ends[0] = step(end_grad, less[1], NT) + give[...]
    rows = []
    for b in range(2):
        back[b], row = block_logit_grads(lg[b : b + 1, :], ends[b], err[b], back0[b], bk[b])
        rows.append(row)
    odd = lax.broadcasted_iota(jnp.int32, (32, L), 0) % 2
    message[...] = jnp.where(odd == 0, rows[0], rows[1])


def kernel_keys(side, lg, held, swapped, start, ends, err, back, dkp, mine, theirs):
    ks = in_order(side, held[0], swapped[0])
    dks = [
        block_key_grads(ks[b], lg[b : b + 1, :], start[b], ends[b], err[b], back[b], dkp[b])
        for b in range(2)
    ]
    for i, pair in enumerate((dks, (back[0], back[1]))):
        x, y = in_order(side, *pair)
        mine[i], theirs[i] = x.astype(BF16), y.astype(BF16)


def kernel_weight(side, slot, got, hidden, swapped, total, grads):
    rows = [got[pl.ds(b, 16, stride=2), :] for b in range(2)]
    here, there = in_order(side, *rows)
    grads[...] = here.astype(BF16)
    theirs = jnp.concatenate([swapped[4], swapped[5]], axis=1)
    weight = dot1(here.astype(BF16), hidden[...]) + dot1(there.astype(BF16), theirs)
    bias = jnp.sum(rows[0] + rows[1], axis=1, keepdims=True)
    row = lax.broadcasted_iota(jnp.int32, (16, 2 * D), 0)
    col = lax.broadcasted_iota(jnp.int32, (16, 2 * D), 1)
    line = jnp.sum(
        jnp.where((row - 2 * slot[0] == col) & (col < 2), bias, 0.0), axis=0, keepdims=True
    )
    for i in range(total.shape[0]):
        total[i, 0:16] = weight
        total[i, 16:24] = jnp.broadcast_to(line, (8, 2 * D))


def added(got):
    parts = [got[i] for i in range(got.shape[0])]
    while len(parts) > 1:
        parts = [sum(parts[i : i + 2]) for i in range(0, len(parts), 2)]
    return parts[0]


def kernel_add(got, total):
    value = added(got)
    for i in range(total.shape[0]):
        total[i] = value


def kernel_last(got, weight, bias):
    value = added(got)
    weight[...] = value[:16]
    bias[...] = value[16:]


VM = pl.BlockSpec(memory_space=pltpu.VMEM)
SM = pl.BlockSpec(memory_space=pltpu.SMEM)


def call(body, outs, *args, flops=1e8):
    specs = [SM if a.ndim == 1 else VM for a in args]
    total = sum(a.size * a.dtype.itemsize for a in args)
    return pl.pallas_call(
        body,
        out_shape=[jax.ShapeDtypeStruct(s, t) for s, t in outs],
        in_specs=specs,
        out_specs=[VM] * len(outs),
        compiler_params=pltpu.CompilerParams(vmem_limit_bytes=16 * 2**20),
        cost_estimate=pl.CostEstimate(flops=int(flops), bytes_accessed=total, transcendentals=0),
    )(*args)


def copies(x, axis):
    count = lax.axis_size(axis)
    return lax.all_to_all(jnp.broadcast_to(x[None], (count,) + x.shape), axis, 0, 0)


def spread(x, axis):
    return copies(x.astype(jnp.float16), axis).astype(F32)


def swap(x):
    return lax.ppermute(x, "zl", [(0, 1), (1, 0)])


def joined(side, mine, theirs):
    return jnp.where(
        side == 0,
        jnp.concatenate([mine, theirs], axis=1),
        jnp.concatenate([theirs, mine], axis=1),
    )


HALF = ((D, D), F32)
PAIR = ((2, D, D), F32)
PAIRB = ((2, L, D), BF16)


def per_device(hidden, beta_weight, beta_bias, queries, keys, values, cotangent):
    rows, pairs = lax.axis_size("y"), lax.axis_size("zh")
    side = lax.axis_index("zl").astype(jnp.int32)
    at_y = lax.axis_index("y").astype(jnp.int32).reshape(1)
    at_z = lax.axis_index("zh").astype(jnp.int32).reshape(1)
    at_s = side.reshape(1)

    at_h = lax.axis_index("head").astype(jnp.int32).reshape(1)

    four, six = [jax.ShapeDtypeStruct((n, L, D), BF16) for n in (4, 6)]
    part, held, theirs = pl.pallas_call(
        kernel_first,
        out_shape=[jax.ShapeDtypeStruct((16, L), F32), four, six],
        in_specs=[SM] * 2 + [pl.BlockSpec(memory_space=pl.ANY)] * 7,
        out_specs=[VM] * 3,
        scratch_shapes=[
            pltpu.SMEM((2,), F32),
            pltpu.VMEM((16, 2 * D), BF16),
            pltpu.VMEM((5, L, 2 * D), BF16),
            pltpu.SemaphoreType.DMA((7,)),
        ],
        compiler_params=pltpu.CompilerParams(vmem_limit_bytes=60 * 2**20),
        cost_estimate=pl.CostEstimate(flops=10**7, bytes_accessed=10**6, transcendentals=0),
    )(at_s, at_h, beta_bias, beta_weight.T, hidden, keys, values, queries, cotangent)
    part = lax.all_to_all(part, ("head", "zl"), 0, 0, tiled=True)
    swapped = swap(theirs)

    send1, logits, less, gain, inv, sk, sv = call(
        kernel_prepare, [((2 * D + 16, D), F32), ((2, L), F32)] + [PAIR] * 5,
        at_s, part, held, swapped,
    )
    got1 = spread(send1, "zh")
    (send2,) = call(
        functools.partial(kernel_row_forward, pairs), [((2 * D + 16, D), F32)], got1
    )
    got2 = spread(send2, "y")
    own1, matrix, read, fixed, bo, bk = call(
        functools.partial(kernel_side, pairs), [((2 * D, D), F32), HALF] + [PAIR] * 4,
        at_z, at_s, logits, held, swapped, got1, inv, sk, sv,
    )
    out, start, draw, give, send3 = call(
        functools.partial(kernel_outputs, rows),
        [PAIRB] + [PAIR] * 2 + [HALF, ((D + 16, D), F32)],
        at_y, at_s, got2, own1, held, swapped, less, gain, read, fixed,
    )
    got3 = spread(send3, "zh")
    mine, theirs, dkp, err, back0 = call(
        kernel_early, [PAIRB, PAIRB] + [PAIR] * 3,
        at_s, logits, held, swapped, start, draw, sk, sv, bo, out,
    )
    send4, own2 = call(
        functools.partial(kernel_row_back, pairs), [((D + 16, D), F32), HALF], at_z, got1, got3
    )
    got4 = spread(send4, "y")
    theirs = swap(theirs)
    ends, back, message = call(
        functools.partial(kernel_grads, rows), [PAIR, PAIR, ((32, L), F32)],
        at_y, got2, got4, matrix, own2, logits, less, give, err, back0, bk,
    )
    mine_kv, theirs_kv = call(
        kernel_keys, [PAIRB, PAIRB],
        at_s, logits, held, swapped, start, ends, err, back, dkp,
    )

    message = lax.all_to_all(message.reshape(16, 2, L), ("head", "zl"), 0, 0)
    total, grads = call(
        kernel_weight, [((pairs, 24, 2 * D), F32), ((16, L), BF16)],
        at_s, at_h, message.reshape(32, L), hidden, swapped,
    )
    total, theirs_kv = lax.optimization_barrier((total, theirs_kv))
    (total,) = call(
        kernel_add, [((rows, 24, 2 * D), F32)], lax.all_to_all(total, "zh", 0, 0), flops=1e6
    )
    d_weight, d_bias = call(
        kernel_last, [((16, 2 * D), F32), ((8, 2 * D), F32)],
        lax.all_to_all(total, "y", 0, 0), flops=1e6,
    )
    theirs_kv = swap(theirs_kv)
    d_hidden = lax.dot_general(
        grads, beta_weight, (((0,), (1,)), ((), ())), preferred_element_type=F32
    )
    out, dq = [joined(side, mine[i], theirs[i]) for i in range(2)]
    dk, dv = [joined(side, mine_kv[i], theirs_kv[i]) for i in range(2)]
    return (out, dq, dk, dv, d_hidden.astype(BF16), d_weight.T, d_bias[0, 0:2])


def solution(mesh):
    grid = Mesh(mesh.devices.reshape(8, 6, 2, 8), ("y", "zh", "zl", "head"))
    seq = P(("y", "zh", "zl"), "head")
    return jax.shard_map(
        per_device,
        mesh=grid,
        in_specs=(seq, P("head", None), P("head"), seq, seq, seq, seq),
        out_specs=(seq, seq, seq, seq, seq, P("head", None), P("head")),
        check_vma=False,
    )
```
